128 devices in a mesh: dp: 16 (over y, z), ep: 8 (over x, core).
Axes of the slice: x: 4, y: 4, z: 4, core: 2. Of those that a mesh axis runs over, the one named last changes fastest.
Arguments:
- hidden_in: bfloat16 [16384, 3584], P(('dp', 'ep')), may hold values from -6 to 6
- query_heads: bfloat16 [16384, 12288], P('dp', 'ep'), may hold values from -256 to 256
- latent_cache: bfloat16 [16, 1536, 576], P('dp'), may hold values from -5 to 5
- prefix_lens: int32 [16], P('dp'), may hold values from 128 to 512, as said below
- latent_up: bfloat16 [512, 16384], P(None, 'ep'), may hold values from -0.25 to 0.25
- head_out: bfloat16 [8192, 3584], P('ep'), may hold values from -0.5 to 0.5
- norm_gain: float32 [3584], replicated, may hold values from 0.25 to 1.75
- expert_ids: int32 [16384, 2], P(('dp', 'ep')), may hold values from 0 to 15, all different within a row; in each aligned block of 128 rows (0 to 127, 128 to 255, ...) at most 17 rows name the same one
- gate_weights: float32 [16384, 2], P(('dp', 'ep')), may hold values from 0.2 to 1
- expert_in: bfloat16 [16, 3584, 2, 2048], P('dp', None, None, 'ep'), may hold values from -0.09375 to 0.09375
- expert_out: bfloat16 [16, 2048, 3584], P('dp', 'ep'), may hold values from -0.125 to 0.125
Outputs:
- layer_out: bfloat16 [16384, 3584], P(('dp', 'ep'))
The draws below stay inside these ranges and needn't reach their ends.
Inputs may be any that keep to these rules, and one draw needn't show every extreme that they name: `prefix_lens`: some rank has exactly 512 prefix positions in every draw. `expert_ids`: within the rows of one device no expert is named by more than 17 rows; each token names 2 different experts.
All inputs are finite; a program needn't handle non-finite values.
Results may differ from the reference program's by a relative error of at most 0.017.
Values may be sent and summed in bfloat16 or wider, within the bound.
No kernel may reach another device: no remote copies, remote signals or barrier semaphores. Data moves between devices by JAX's collectives and lax.ppermute only.
A program may use at most 192 MiB of HBM per device.

```python
import math
import jax
import jax.numpy as jnp
import numpy as np
from jax import lax

D = 3584
H = 64
NOPE = 128
ROPE = 64
VDIM = 128
LAT = 512
FF = 2048
TOP = 2
TOK_DEV = 128
PMAX = 512
SPAN = 1024
TOKENS = 16384
KEYS = 1536
EXPERTS = 16
CAP = 17
N_DP = 16
N_EP = 8
DEVICES = 128


def shared_latent(key):
    base = jnp.clip(jax.random.normal(key, (N_DP, KEYS, LAT + ROPE), jnp.float32), -4.0, 4.0)
    return base


def draw_latent_cache(key, part):
    base = shared_latent(key)
    return base.astype(jnp.bfloat16)


def draw_query_heads(key, part):
    key = jax.random.fold_in(key, 7)
    queries = jnp.clip(jax.random.normal(key, (TOKENS, H, NOPE + ROPE), jnp.float32), -5.0, 5.0)
    return queries.reshape(TOKENS, H * (NOPE + ROPE)).astype(jnp.bfloat16)


def draw_prefix_lens(key, part):
    key = jax.random.fold_in(key, 5)
    lengths = jax.random.randint(key, (N_DP,), PMAX // 4, PMAX + 1)
    longest = jax.random.randint(jax.random.fold_in(key, 1), (), 0, N_DP)
    return jnp.where(jnp.arange(N_DP) == longest, PMAX, lengths).astype(jnp.int32)


def shard_levels(stream_key, extent, pieces, least, top_value):
    def one(position, parts):
        draws = jax.random.uniform(jax.random.fold_in(jax.random.fold_in(stream_key, 6), position), (parts,), jnp.float32, least / len(pieces), top_value / len(pieces))
        return jnp.repeat(jnp.exp(draws), extent[position] // parts).reshape((-1,) + (1,) * (len(extent) - position - 1))

    factor_of = one(*pieces[0])
    for cut in pieces[1:]:
        factor_of = factor_of * one(*cut)
    return factor_of


def deal_out(stream_key, own, number, rows, count, top, limit, slope):
    order = jax.random.permutation(stream_key, count)
    crowded, usual = load_shares(count, rows * top, limit, slope, True), load_shares(count, rows * top, limit, slope, False)
    places = jnp.arange(count)

    def named(sizes, offset_by):
        used = int((sizes > 0).sum())
        fixed = max(1, used // 4)
        moved = fixed + (places - fixed + offset_by * (used - fixed)) % max(1, count - fixed)
        return jnp.zeros((count,), jnp.int32).at[order[jnp.where(places < fixed, places, moved)]].set(jnp.asarray(sizes, jnp.int32))

    sizes = jnp.where(number % 4 == 0, named(crowded, number // 4), named(usual, number - number // 4 - 1))
    mixed = jax.random.permutation(jax.random.fold_in(own, 3), count)
    donor, taker = mixed[0:count // 2 * 2:2], mixed[1:count // 2 * 2:2]
    room = jnp.minimum(sizes[donor] - 1, limit - sizes[taker]) // 2
    room = jnp.where((donor == order[0]) | (taker == order[0]) | (sizes[taker] == 0), 0, jnp.maximum(room, 0))
    moved = jax.random.randint(jax.random.fold_in(own, 4), (count // 2,), 0, 1 << 20) % (room + 1)
    sizes = sizes.at[donor].add(-moved).at[taker].add(moved)
    members = jnp.searchsorted(jnp.cumsum(sizes), jnp.arange(rows * top), side="right").astype(jnp.int32)
    listing = members.reshape(top, rows).T
    listing = listing[jax.random.permutation(jax.random.fold_in(own, 1), rows)]
    offset_by = jax.random.randint(jax.random.fold_in(own, 2), (rows, 1), 0, top)
    return jnp.take_along_axis(listing, (jnp.arange(top)[None, :] + offset_by) % top, axis=1)


def load_shares(count, total, limit, skew, full):
    loads = [(1 << 20) // math.isqrt(standing ** skew) + 1 for standing in range(1, count + 1)]
    largest = limit if full else min(limit, max(-(-total // count), total * loads[0] // sum(loads)))
    least = 1 if total - largest >= count - 1 else 0
    counts, spare = [largest] + [least] * (count - 1), total - largest - least * (count - 1)
    while spare > 0:
        candidates = [i for i in range(1, count) if counts[i] < largest] or [i for i in range(1, count) if counts[i] < limit]
        whole, left = sum([loads[i] for i in candidates]), spare
        for i in candidates:
            extra = min(limit - counts[i], max(1, left * loads[i] // whole), spare)
            counts[i] = counts[i] + extra
            spare = spare - extra
    return np.array(counts)


def scatter_about(own_key, shape, width, limit, cuts=(), held_as=jnp.bfloat16):
    values = jax.random.normal(own_key, shape, jnp.float32) * width
    if len(cuts) > 0:
        values = shard_levels(own_key, shape, cuts, -0.22, 0.18) * values
    return jnp.clip(values, min=-limit, max=limit).astype(held_as)


def setup_inputs(seed: int = 0) -> dict:
    seeds = jax.random.split(jax.random.key(seed), 12)
    hidden_in = scatter_about(seeds[0], (TOKENS, D), 1.0, 6.0, ((0, 128),))
    query_heads = draw_query_heads(jax.random.fold_in(seeds[11], 71), 0)
    latent_cache = draw_latent_cache(jax.random.fold_in(seeds[11], 71), 0)
    prefix_lens = draw_prefix_lens(jax.random.fold_in(seeds[11], 71), 0)
    latent_up = scatter_about(seeds[4], (LAT, H * (NOPE + VDIM)), LAT ** -0.5, 0.25, ((1, 8),))
    head_out = scatter_about(seeds[5], (H * VDIM, D), (max(1, H * VDIM // 64)) ** -0.5, 0.5, ((0, 8),))
    norm_gain = jnp.clip(1.0 + 0.15 * jax.random.normal(seeds[6], (D,), jnp.float32), 0.25, 1.75)
    expert_ids_keys = jax.random.split(jax.random.fold_in(seeds[7], 1), TOKENS // TOK_DEV)
    expert_ids_turns = jax.random.permutation(jax.random.fold_in(seeds[7], 3), TOKENS // TOK_DEV)
    expert_ids = jax.vmap(lambda own, number: deal_out(jax.random.fold_in(seeds[7], 2), own, number, TOK_DEV, EXPERTS, TOP, CAP, 2))(expert_ids_keys, expert_ids_turns).reshape((TOKENS, TOP))
    gate_weights = jnp.clip(0.2 + 0.8 * jax.random.uniform(seeds[8], (TOKENS, TOP), jnp.float32) ** shard_levels(seeds[8], (TOKENS, TOP), ((0, 128),), -0.2, 0.2), 0.2, 1.0)
    expert_in = scatter_about(seeds[9], (EXPERTS, D, 2, FF), D ** -0.5, 0.09375, ((0, 16), (3, 8)))
    expert_out = scatter_about(seeds[10], (EXPERTS, FF, D), FF ** -0.5, 0.125, ((0, 16), (1, 8)))
    return {"hidden_in": hidden_in, "query_heads": query_heads, "latent_cache": latent_cache, "prefix_lens": prefix_lens, "latent_up": latent_up, "head_out": head_out, "norm_gain": norm_gain, "expert_ids": expert_ids, "gate_weights": gate_weights, "expert_in": expert_in, "expert_out": expert_out}


def reference(hidden_in, query_heads, latent_cache, prefix_lens, latent_up, head_out, norm_gain, expert_ids, gate_weights, expert_in, expert_out):
    score_scale = (NOPE + ROPE) ** (-0.5)
    key_pos = jnp.arange(KEYS)
    query_pos = jnp.arange(SPAN)
    group_heads = H // N_EP

    def rank_attention(inputs):
        query_rank, latent_rows, prefix_len = inputs
        unpacked = jnp.dot(latent_rows[:, :LAT], latent_up, preferred_element_type=jnp.float32).astype(jnp.bfloat16)
        unpacked = unpacked.reshape(KEYS, H, NOPE + VDIM).astype(jnp.float32)
        queries = query_rank.reshape(SPAN, H, NOPE + ROPE).astype(jnp.float32)
        rotary = latent_rows[:, LAT:].astype(jnp.float32)
        scores = jnp.einsum('chn,khn->hck', queries[..., :NOPE], unpacked[..., :NOPE])
        scores = scores + jnp.einsum('chr,kr->hck', queries[..., NOPE:], rotary)
        scores = scores * score_scale
        visible = jnp.where(key_pos[None, :] < PMAX, key_pos[None, :] < prefix_len, key_pos[None, :] - PMAX <= query_pos[:, None])
        scores = jnp.where(visible[None], scores, -1e+30)
        row_peak = lax.optimization_barrier(jnp.max(scores, -1, keepdims=True))
        exp_scores = jnp.exp(scores - row_peak)
        weights_bf = (exp_scores / lax.optimization_barrier(jnp.sum(exp_scores, -1, keepdims=True))).astype(jnp.bfloat16)
        attended = jnp.einsum('hck,khv->chv', weights_bf.astype(jnp.float32), unpacked[..., NOPE:]).astype(jnp.bfloat16)
        attended = attended.reshape(SPAN, N_EP, group_heads * VDIM).astype(jnp.float32)
        group_terms = jnp.einsum('cgv,gvd->gcd', attended, head_out.reshape(N_EP, group_heads * VDIM, D).astype(jnp.float32))
        group_terms = lax.optimization_barrier(group_terms.astype(jnp.bfloat16)).astype(jnp.float32)
        return lax.optimization_barrier(jnp.sum(group_terms, 0))
    attention = lax.map(rank_attention, (query_heads.reshape(N_DP, SPAN, H * (NOPE + ROPE)), latent_cache, prefix_lens))
    attention = attention.reshape(TOKENS, D)
    stream = hidden_in.astype(jnp.float32) + attention
    normed = (stream * lax.rsqrt(lax.optimization_barrier(jnp.mean(stream * stream, -1, keepdims=True)) + 1e-06) * norm_gain).astype(jnp.bfloat16)
    device_ids = expert_ids.reshape(DEVICES, TOK_DEV * TOP)
    one_hot = (device_ids[:, :, None] == jnp.arange(EXPERTS, dtype=jnp.int32)[None, None, :]).astype(jnp.int32)
    slot_index = lax.optimization_barrier(jnp.sum((jnp.cumsum(one_hot, 1) - 1) * one_hot, -1)).astype(jnp.int32)
    slot_rows = (jnp.arange(DEVICES, dtype=jnp.int32)[:, None] * CAP + slot_index).reshape(TOKENS, TOP).astype(jnp.int32)
    sources = jnp.broadcast_to(normed[:, None, :], (TOKENS, TOP, D))
    buffers = jnp.zeros((EXPERTS, DEVICES * CAP, D), jnp.bfloat16).at[expert_ids, slot_rows].set(sources)
    group_units = FF // N_EP

    def run_expert(inputs):
        rows_in, weights_in, weights_out = inputs
        gate = jnp.dot(rows_in, weights_in[:, 0, :], preferred_element_type=jnp.float32)
        upper = jnp.dot(rows_in, weights_in[:, 1, :], preferred_element_type=jnp.float32)
        active = (jax.nn.silu(gate) * upper).astype(jnp.bfloat16)
        active = active.reshape(DEVICES * CAP, N_EP, group_units).astype(jnp.float32)
        group_terms = jnp.einsum('rgf,gfd->grd', active, weights_out.reshape(N_EP, group_units, D).astype(jnp.float32))
        group_terms = lax.optimization_barrier(group_terms.astype(jnp.bfloat16)).astype(jnp.float32)
        return lax.optimization_barrier(jnp.sum(group_terms, 0))
    expert_value = lax.map(run_expert, (buffers, expert_in, expert_out))
    picked = expert_value[expert_ids, slot_rows]
    expert_mix = lax.optimization_barrier(jnp.sum(picked * gate_weights[:, :, None], 1))
    return (stream + expert_mix).astype(jnp.bfloat16)
```

```python
import functools

import jax
import jax.numpy as jnp
from jax import lax
from jax.experimental import pallas as pl
from jax.experimental.pallas import tpu as pltpu
from jax.sharding import PartitionSpec as P

NOPE = 128
ROPE = 64
VDIM = 128
LAT = 512
PMAX = 512
SLOTS = 16
BF = jnp.bfloat16
F32 = jnp.float32
VMEM = 56 * 1024 * 1024


def dot(a, b):
    return jnp.dot(a, b, preferred_element_type=F32)


def keys_kernel(latent_ref, up_ref, keys_ref, values_ref):
    rows = latent_ref.shape[0]
    lat = latent_ref[:, :LAT]
    rot = latent_ref[:, LAT:].astype(F32)
    rot = jnp.concatenate([rot, jnp.zeros((rows, 128 - ROPE), F32)], 1)
    low = lax.broadcasted_iota(jnp.int32, (rows, 128), 1) < 64
    even = dot(lat, up_ref[:, :256])
    keys_ref[0, :, :128] = even[:, :128].astype(BF)
    keys_ref[0, :, 128:] = rot.astype(BF)
    values_ref[0] = even[:, 128:].astype(BF)
    odd = dot(lat, up_ref[:, 256:])
    turned = pltpu.roll(odd[:, :128], 64, 1)
    keys_ref[1, :, :128] = jnp.where(low, 0.0, turned).astype(BF)
    keys_ref[1, :, 128:] = jnp.where(low, turned, pltpu.roll(rot, 64, 1)).astype(BF)
    values_ref[1] = odd[:, 128:].astype(BF)


def make_keys(latent, up):
    rows = latent.shape[0]
    heads = up.shape[1] // (NOPE + VDIM)
    return pl.pallas_call(
        keys_kernel,
        grid=(heads // 2,),
        in_specs=[
            pl.BlockSpec((rows, latent.shape[1]), lambda p: (0, 0)),
            pl.BlockSpec((LAT, 512), lambda p: (0, p)),
        ],
        out_specs=[
            pl.BlockSpec((2, rows, 256), lambda p: (p, 0, 0)),
            pl.BlockSpec((2, rows, 128), lambda p: (p, 0, 0)),
        ],
        out_shape=[
            jax.ShapeDtypeStruct((heads, rows, 256), BF),
            jax.ShapeDtypeStruct((heads, rows, 128), BF),
        ],
        compiler_params=pltpu.CompilerParams(vmem_limit_bytes=VMEM),
        name="make_keys",
    )(latent, up)


def attend_kernel(info_ref, q_ref, keys_ref, values_ref, out_w_ref, keep_ref, send_ref, acc_ref):
    pair = pl.program_id(0)
    block = info_ref[0]
    core = info_ref[1]
    prefix_len = info_ref[2]
    qb = q_ref.shape[0]
    factor = (NOPE + ROPE) ** (-0.5) * 1.4426950408889634
    ones = jnp.ones((qb, 128), BF)

    @pl.when(pair == 0)
    def _():
        acc_ref[...] = jnp.zeros_like(acc_ref)

    def one_head(h, count):
        q = q_ref[:, h * 128 : h * 128 + 256]
        scores = []
        for t in range(PMAX // qb + count):
            s = lax.dot_general(
                q,
                keys_ref[h, t * qb : (t + 1) * qb, :],
                (((1,), (1,)), ((), ())),
                preferred_element_type=F32,
            )
            col = lax.broadcasted_iota(jnp.int32, (qb, qb), 1)
            if t < PMAX // qb:
                s = jnp.where(col + t * qb < prefix_len, s, -1e30)
            elif t == PMAX // qb + count - 1:
                row = lax.broadcasted_iota(jnp.int32, (qb, qb), 0)
                s = jnp.where(col <= row, s, -1e30)
            scores.append(s)
        peak = functools.reduce(jnp.maximum, scores)
        peak = jnp.max(peak, 1, keepdims=True)
        total = jnp.zeros((qb, 256), F32)
        for t, s in enumerate(scores):
            p = jnp.exp2((s - peak) * factor).astype(BF)
            v = values_ref[h, t * qb : (t + 1) * qb, :]
            total = total + dot(p, jnp.concatenate([v, ones], 1))
        return (total[:, :128] / total[:, 128:]).astype(BF)

    for b in range(4):

        @pl.when(block == b)
        def _(b=b):
            o = jnp.concatenate([one_head(0, b + 1), one_head(1, b + 1)], 1)
            acc_ref[...] += dot(o, out_w_ref[...])

    @pl.when(pair == pl.num_programs(0) - 1)
    def _():
        half = qb // 2
        keep_ref[...] = acc_ref[pl.ds(pl.multiple_of(core * half, half), half), :].astype(BF)
        send_ref[...] = acc_ref[pl.ds(pl.multiple_of((1 - core) * half, half), half), :].astype(BF)


def attend_block(info, queries, keys, values, out_w):
    rows = keys.shape[1]
    width = out_w.shape[1]
    qb = 256
    return pl.pallas_call(
        attend_kernel,
        grid_spec=pltpu.PrefetchScalarGridSpec(
            num_scalar_prefetch=1,
            grid=(keys.shape[0] // 2,),
            in_specs=[
                pl.BlockSpec((qb, 384), lambda p, info: (info[0], p)),
                pl.BlockSpec((2, rows, 256), lambda p, info: (p, 0, 0)),
                pl.BlockSpec((2, rows, 128), lambda p, info: (p, 0, 0)),
                pl.BlockSpec((256, width), lambda p, info: (p, 0)),
            ],
            out_specs=[
                pl.BlockSpec((qb // 2, width), lambda p, info: (0, 0)),
                pl.BlockSpec((qb // 2, width), lambda p, info: (0, 0)),
            ],
            scratch_shapes=[pltpu.VMEM((qb, width), F32)],
        ),
        out_shape=[jax.ShapeDtypeStruct((qb // 2, width), BF)] * 2,
        compiler_params=pltpu.CompilerParams(vmem_limit_bytes=VMEM),
        name="attend_block",
    )(info, queries, keys, values, out_w)


def pack(main, extra, spare_ref, msg_refs):
    experts = msg_refs[0].shape[0]
    spare_ref[...] = jnp.zeros_like(spare_ref)
    per = main.shape[1] // 128 // len(msg_refs)
    for i, msg in enumerate(msg_refs):
        for c in range(per):
            lanes = slice((i * per + c) * 128, (i * per + c + 1) * 128)
            msg[:, c * SLOTS : (c + 1) * SLOTS, :] = (
                main[:, lanes].astype(BF).reshape(experts, SLOTS, 128)
            )
            spare_ref[:, i * 16 + c, :] = extra[:, lanes].astype(F32)
        msg[:, per * SLOTS :, :] = spare_ref[:, i * 16 : (i + 1) * 16, :].astype(BF)


def unpack(msg_refs, spare_ref, rows_ref):
    experts = msg_refs[0].shape[0]
    main = experts * SLOTS
    per = rows_ref.shape[1] // 128 // len(msg_refs)
    for i, msg in enumerate(msg_refs):
        spare_ref[:, i * 16 : (i + 1) * 16, :] = msg[:, per * SLOTS :, :].astype(F32)
        for c in range(per):
            lanes = slice((i * per + c) * 128, (i * per + c + 1) * 128)
            rows_ref[:main, lanes] = msg[:, c * SLOTS : (c + 1) * SLOTS, :].reshape(main, 128)
            rows_ref[main : main + experts, lanes] = spare_ref[:, i * 16 + c, :].astype(BF)


def dispatch_kernel(
    hidden_ref, own_ref, own_core_ref, r1_ref, r2_ref, r3_ref, gain_ref, ids_ref,
    stream_ref, msg_a_ref, msg_b_ref, spare_ref,
):
    rows = hidden_ref.shape[0]
    experts = msg_a_ref.shape[0]
    stream = hidden_ref[...].astype(F32)
    for ref in (own_ref, own_core_ref, r1_ref, r2_ref, r3_ref):
        stream = stream + ref[...].astype(F32)
    stream_ref[...] = stream
    mean = jnp.mean(stream * stream, -1, keepdims=True)
    normed = (stream * lax.rsqrt(mean + 1e-6) * gain_ref[...]).astype(BF)
    before = (
        lax.broadcasted_iota(jnp.int32, (rows, rows), 0)
        < lax.broadcasted_iota(jnp.int32, (rows, rows), 1)
    ).astype(BF)

    def picks(count, expert, slot):
        named = (ids_ref[0:1, :] == expert) | (ids_ref[1:2, :] == expert)
        earlier = dot(named.astype(F32).astype(BF), before)
        return jnp.where(named & (earlier == slot.astype(F32)), 1.0, 0.0).astype(BF)

    line = lax.broadcasted_iota(jnp.int32, (experts * SLOTS, rows), 0)
    main = dot(picks(experts * SLOTS, line // SLOTS, line % SLOTS), normed)
    line = lax.broadcasted_iota(jnp.int32, (experts, rows), 0)
    extra = dot(picks(experts, line, jnp.full((experts, rows), SLOTS, jnp.int32)), normed)
    pack(main, extra, spare_ref, (msg_a_ref, msg_b_ref))


def dispatch(hidden, own, own_core, r1, r2, r3, gain, ids_t, experts):
    rows, width = hidden.shape
    message = jax.ShapeDtypeStruct((experts, width // 256 * SLOTS + 16, 128), BF)
    return pl.pallas_call(
        dispatch_kernel,
        out_shape=[jax.ShapeDtypeStruct((rows, width), F32), message, message],
        scratch_shapes=[pltpu.VMEM((experts, 32, 128), F32)],
        compiler_params=pltpu.CompilerParams(vmem_limit_bytes=VMEM),
        name="dispatch",
    )(hidden, own, own_core, r1, r2, r3, gain.reshape(1, width), ids_t)


def expert_kernel(n, *refs):
    msgs, refs = refs[:2], refs[2:]
    w_in, refs = refs[:n], refs[n:]
    w_out, refs = refs[:n], refs[n:]
    outs, refs = refs[:2], refs[2:]
    rows_ref, spare_ref, in_buf, out_buf, sems = refs
    copies = []
    for s in range(n):
        pair = (
            pltpu.make_async_copy(w_in[s], in_buf.at[s], sems.at[0, s]),
            pltpu.make_async_copy(w_out[s], out_buf.at[s], sems.at[1, s]),
        )
        for copy in pair:
            copy.start()
        copies.append(pair)
    unpack(msgs, spare_ref, rows_ref)
    units = out_buf.shape[1]
    total = None
    for s in range(n):
        copies[s][0].wait()
        joined = dot(rows_ref[...], in_buf[s])
        gate, up = joined[:, :units], joined[:, units:]
        active = (gate / (1.0 + jnp.exp(-gate)) * up).astype(BF)
        copies[s][1].wait()
        part = dot(active, out_buf[s])
        total = part if total is None else total + part
    experts = outs[0].shape[0]
    main = experts * SLOTS
    pack(total[:main], total[main:], spare_ref, outs)


def run_expert(msgs, w_in, w_out):
    n = len(w_in)
    experts = msgs[0].shape[0]
    width = w_out[0].shape[1]
    rows = experts * (SLOTS + 1)
    return pl.pallas_call(
        functools.partial(expert_kernel, n),
        in_specs=[pl.BlockSpec(memory_space=pltpu.VMEM)] * 2 + [pl.BlockSpec(memory_space=pl.ANY)] * (2 * n),
        out_specs=[pl.BlockSpec(memory_space=pltpu.VMEM)] * 2,
        out_shape=[jax.ShapeDtypeStruct(m.shape, BF) for m in msgs],
        scratch_shapes=[
            pltpu.VMEM((rows, width), BF),
            pltpu.VMEM((experts, 32, 128), F32),
            pltpu.VMEM((n,) + w_in[0].shape, BF),
            pltpu.VMEM((n,) + w_out[0].shape, BF),
            pltpu.SemaphoreType.DMA((2, n)),
        ],
        compiler_params=pltpu.CompilerParams(vmem_limit_bytes=VMEM),
        name="run_expert",
    )(*msgs, *w_in, *w_out)


def combine_kernel(stream_ref, msg_a_ref, msg_b_ref, ids_ref, gates_ref, out_ref, rows_ref, spare_ref):
    rows = stream_ref.shape[0]
    experts = msg_a_ref.shape[0]
    main = experts * SLOTS
    rows_ref[main:, :] = jnp.zeros((128, rows_ref.shape[1]), BF)
    unpack((msg_a_ref, msg_b_ref), spare_ref, rows_ref)
    before = (
        lax.broadcasted_iota(jnp.int32, (rows, rows), 1)
        < lax.broadcasted_iota(jnp.int32, (rows, rows), 0)
    ).astype(BF)
    place = lax.broadcasted_iota(jnp.int32, (rows, main + 128), 1)
    expert = jnp.where(place < main, place // SLOTS, place - main)
    slot = jnp.where(place < main, place % SLOTS, SLOTS)
    first = ids_ref[:, 0:1] == expert
    second = ids_ref[:, 1:2] == expert
    named = jnp.where(first | second, 1.0, 0.0).astype(BF)
    earlier = dot(before, named)
    weight = jnp.where(first, gates_ref[:, 0:1], jnp.where(second, gates_ref[:, 1:2], 0.0))
    weight = jnp.where(earlier == slot.astype(F32), weight, 0.0)
    mix = stream_ref[...]
    for _ in range(3):
        part = weight.astype(BF)
        mix = mix + dot(part, rows_ref[...])
        weight = weight - part.astype(F32)
    out_ref[...] = mix.astype(BF)


def combine(stream, msgs, ids, gates):
    rows, width = stream.shape
    experts = msgs[0].shape[0]
    return pl.pallas_call(
        combine_kernel,
        out_shape=jax.ShapeDtypeStruct((rows, width), BF),
        scratch_shapes=[
            pltpu.VMEM((experts * SLOTS + 128, width), BF),
            pltpu.VMEM((experts, 32, 128), F32),
        ],
        compiler_params=pltpu.CompilerParams(vmem_limit_bytes=VMEM),
        name="combine",
    )(stream, *msgs, ids, gates)


def shards(
    hidden_in,
    query_heads,
    latent_cache,
    prefix_lens,
    latent_up,
    head_out,
    norm_gain,
    expert_ids,
    gate_weights,
    expert_in,
    expert_out,
):
    experts = lax.axis_size("dp")
    group = lax.axis_size("ep")
    chips = group // 2
    place = lax.axis_index("ep")
    chip, core = place // 2, place % 2

    def to_chip(x, target):
        pairs = [(i, 2 * target(i // 2) + i % 2) for i in range(group)]
        return lax.ppermute(x, "ep", pairs)

    def to_core(x):
        return lax.ppermute(x, "ep", [(i, i ^ 1) for i in range(group)])

    model_width = expert_in.shape[1]
    w_in = expert_in.reshape(model_width, -1)
    w_out = expert_out[0]
    w_out_pair = to_chip(w_out, lambda x: x ^ 1)
    w_in_pair = to_chip(w_in, lambda x: x ^ 1)
    w_ins = (w_in, to_core(w_in), w_in_pair, to_core(w_in_pair))
    w_outs = (w_out, to_core(w_out), w_out_pair, to_core(w_out_pair))

    keys, values = make_keys(latent_cache[0], latent_up)
    sums = {}
    for step in (1, 2, 3, 0):
        info = jnp.stack([(chip + step) % chips, core, prefix_lens[0]]).astype(jnp.int32)
        keep, send = attend_block(info, query_heads, keys, values, head_out)
        sums[step] = (keep, to_core(send))
    arrived = []
    for step in (1, 2, 3):
        block = (sums[step][0].astype(F32) + sums[step][1].astype(F32)).astype(BF)
        arrived.append(to_chip(block, lambda x, step=step: (x + step) % chips))
    stream, *msgs = dispatch(
        hidden_in, *sums[0], *arrived, norm_gain, expert_ids.T, experts
    )
    exchange = lambda m: lax.all_to_all(m, "dp", split_axis=0, concat_axis=0, tiled=True)
    other = lambda x: chips - 1 - x
    mine = [exchange(m) for m in msgs]
    theirs = [to_chip(m, other) for m in mine]
    mine_out = run_expert(mine, w_ins, w_outs)
    theirs_out = run_expert(theirs, w_ins, w_outs)
    back = [to_chip(m, other) for m in theirs_out]
    home = [
        exchange((a.astype(F32) + b.astype(F32)).astype(BF)) for a, b in zip(mine_out, back)
    ]
    return combine(stream, home, expert_ids, gate_weights)


def solution(mesh):
    in_specs = (
        P(("dp", "ep"), None),
        P("dp", "ep"),
        P("dp", None, None),
        P("dp"),
        P(None, "ep"),
        P("ep", None),
        P(),
        P(("dp", "ep"), None),
        P(("dp", "ep"), None),
        P("dp", None, None, "ep"),
        P("dp", "ep", None),
    )
    out_specs = P(("dp", "ep"), None)
    return jax.shard_map(shards, mesh=mesh, in_specs=in_specs, out_specs=out_specs, check_vma=False)
```

```python
import functools

import jax
import jax.numpy as jnp
from jax import lax
from jax.experimental import pallas as pl
from jax.experimental.pallas import tpu as pltpu
from jax.sharding import PartitionSpec as P

NOPE = 128
ROPE = 64
VDIM = 128
LAT = 512
PMAX = 512
SLOTS = 16
BF = jnp.bfloat16
F32 = jnp.float32
VMEM = 56 * 1024 * 1024
COST = pl.CostEstimate(flops=4_000_000_000, transcendentals=0, bytes_accessed=1_000_000)


def dot(a, b):
    return jnp.dot(a, b, preferred_element_type=F32)


def keys_kernel(latent_ref, up_ref, *refs):
    keys_ref, values_ref = refs[-2:]
    rows = latent_ref.shape[0]
    lat = latent_ref[:, :LAT]
    rot = latent_ref[:, LAT:].astype(F32)
    rot = jnp.concatenate([rot, jnp.zeros((rows, 128 - ROPE), F32)], 1)
    low = lax.broadcasted_iota(jnp.int32, (rows, 128), 1) < 64
    even = dot(lat, up_ref[:, :256])
    keys_ref[0, :, :128] = even[:, :128].astype(BF)
    keys_ref[0, :, 128:] = rot.astype(BF)
    values_ref[0] = even[:, 128:].astype(BF)
    odd = dot(lat, up_ref[:, 256:])
    turned = pltpu.roll(odd[:, :128], 64, 1)
    keys_ref[1, :, :128] = jnp.where(low, 0.0, turned).astype(BF)
    keys_ref[1, :, 128:] = jnp.where(low, turned, pltpu.roll(rot, 64, 1)).astype(BF)
    values_ref[1] = odd[:, 128:].astype(BF)


def make_keys(latent, up, earlier):
    rows = latent.shape[0]
    heads = up.shape[1] // (NOPE + VDIM)
    return pl.pallas_call(
        keys_kernel,
        grid=(heads // 2,),
        in_specs=[
            pl.BlockSpec((rows, latent.shape[1]), lambda p: (0, 0)),
            pl.BlockSpec((LAT, 512), lambda p: (0, p)),
        ]
        + [pl.BlockSpec(memory_space=pl.ANY)] * len(earlier),
        out_specs=[
            pl.BlockSpec((2, rows, 256), lambda p: (p, 0, 0)),
            pl.BlockSpec((2, rows, 128), lambda p: (p, 0, 0)),
        ],
        out_shape=[
            jax.ShapeDtypeStruct((heads, rows, 256), BF),
            jax.ShapeDtypeStruct((heads, rows, 128), BF),
        ],
        compiler_params=pltpu.CompilerParams(vmem_limit_bytes=VMEM),
        cost_estimate=COST,
        name="make_keys",
    )(latent, up, *earlier)


def attend_kernel(info_ref, q_ref, keys_ref, values_ref, out_w_ref, *refs):
    keep_ref, send_ref, acc_ref = refs[-3:]
    pair = pl.program_id(0)
    block = info_ref[0]
    core = info_ref[1]
    prefix_len = info_ref[2]
    qb = q_ref.shape[0]
    factor = (NOPE + ROPE) ** (-0.5) * 1.4426950408889634
    ones = jnp.ones((qb, 128), BF)

    @pl.when(pair == 0)
    def _():
        acc_ref[...] = jnp.zeros_like(acc_ref)

    def one_head(h, count):
        q = q_ref[:, h * 128 : h * 128 + 256]
        scores = []
        for t in range(PMAX // qb + count):
            s = lax.dot_general(
                q,
                keys_ref[h, t * qb : (t + 1) * qb, :],
                (((1,), (1,)), ((), ())),
                preferred_element_type=F32,
            )
            col = lax.broadcasted_iota(jnp.int32, (qb, qb), 1)
            if t < PMAX // qb:
                s = jnp.where(col + t * qb < prefix_len, s, -1e30)
            elif t == PMAX // qb + count - 1:
                row = lax.broadcasted_iota(jnp.int32, (qb, qb), 0)
                s = jnp.where(col <= row, s, -1e30)
            scores.append(s)
        peak = functools.reduce(jnp.maximum, scores)
        peak = jnp.max(peak, 1, keepdims=True)
        total = jnp.zeros((qb, 256), F32)
        for t, s in enumerate(scores):
            p = jnp.exp2((s - peak) * factor).astype(BF)
            v = values_ref[h, t * qb : (t + 1) * qb, :]
            total = total + dot(p, jnp.concatenate([v, ones], 1))
        return (total[:, :128] / total[:, 128:]).astype(BF)

    for b in range(4):

        @pl.when(block == b)
        def _(b=b):
            o = jnp.concatenate([one_head(0, b + 1), one_head(1, b + 1)], 1)
            acc_ref[...] += dot(o, out_w_ref[...])

    @pl.when(pair == pl.num_programs(0) - 1)
    def _():
        half = qb // 2
        keep_ref[...] = acc_ref[pl.ds(pl.multiple_of(core * half, half), half), :].astype(BF)
        send_ref[...] = acc_ref[pl.ds(pl.multiple_of((1 - core) * half, half), half), :].astype(BF)


def attend_block(info, queries, keys, values, out_w, earlier):
    rows = keys.shape[1]
    width = out_w.shape[1]
    qb = 256
    return pl.pallas_call(
        attend_kernel,
        grid_spec=pltpu.PrefetchScalarGridSpec(
            num_scalar_prefetch=1,
            grid=(keys.shape[0] // 2,),
            in_specs=[
                pl.BlockSpec((qb, 384), lambda p, info: (info[0], p)),
                pl.BlockSpec((2, rows, 256), lambda p, info: (p, 0, 0)),
                pl.BlockSpec((2, rows, 128), lambda p, info: (p, 0, 0)),
                pl.BlockSpec((256, width), lambda p, info: (p, 0)),
            ]
            + [pl.BlockSpec(memory_space=pl.ANY)] * len(earlier),
            out_specs=[
                pl.BlockSpec((qb // 2, width), lambda p, info: (0, 0)),
                pl.BlockSpec((qb // 2, width), lambda p, info: (0, 0)),
            ],
            scratch_shapes=[pltpu.VMEM((qb, width), F32)],
        ),
        out_shape=[jax.ShapeDtypeStruct((qb // 2, width), BF)] * 2,
        compiler_params=pltpu.CompilerParams(vmem_limit_bytes=VMEM),
        cost_estimate=COST,
        name="attend_block",
    )(info, queries, keys, values, out_w, *earlier)


def pack(main, extra, spare_ref, msg_refs):
    experts = msg_refs[0].shape[0]
    spare_ref[...] = jnp.zeros_like(spare_ref)
    per = main.shape[1] // 128 // len(msg_refs)
    for i, msg in enumerate(msg_refs):
        for c in range(per):
            lanes = slice((i * per + c) * 128, (i * per + c + 1) * 128)
            msg[:, c * SLOTS : (c + 1) * SLOTS, :] = (
                main[:, lanes].astype(BF).reshape(experts, SLOTS, 128)
            )
            spare_ref[:, i * 16 + c, :] = extra[:, lanes].astype(F32)
        msg[:, per * SLOTS :, :] = spare_ref[:, i * 16 : (i + 1) * 16, :].astype(BF)


def unpack(msg_refs, spare_ref, rows_ref):
    experts = msg_refs[0].shape[0]
    main = experts * SLOTS
    per = rows_ref.shape[1] // 128 // len(msg_refs)
    for i, msg in enumerate(msg_refs):
        spare_ref[:, i * 16 : (i + 1) * 16, :] = msg[:, per * SLOTS :, :].astype(F32)
        for c in range(per):
            lanes = slice((i * per + c) * 128, (i * per + c + 1) * 128)
            rows_ref[:main, lanes] = msg[:, c * SLOTS : (c + 1) * SLOTS, :].reshape(main, 128)
            rows_ref[main : main + experts, lanes] = spare_ref[:, i * 16 + c, :].astype(BF)


def dispatch_kernel(
    hidden_ref, own_ref, own_core_ref, r1_ref, r2_ref, gain_ref, ids_ref, *refs
):
    stream_ref, msg_a_ref, msg_b_ref, spare_ref = refs[-4:]
    rows = hidden_ref.shape[0]
    experts = msg_a_ref.shape[0]
    stream = hidden_ref[...].astype(F32)
    for ref in (own_ref, own_core_ref, r1_ref, r2_ref):
        stream = stream + ref[...].astype(F32)
    stream_ref[...] = stream
    mean = jnp.mean(stream * stream, -1, keepdims=True)
    normed = (stream * lax.rsqrt(mean + 1e-6) * gain_ref[...]).astype(BF)
    before = (
        lax.broadcasted_iota(jnp.int32, (rows, rows), 0)
        < lax.broadcasted_iota(jnp.int32, (rows, rows), 1)
    ).astype(BF)

    def picks(count, expert, slot):
        named = (ids_ref[0:1, :] == expert) | (ids_ref[1:2, :] == expert)
        earlier = dot(named.astype(F32).astype(BF), before)
        return jnp.where(named & (earlier == slot.astype(F32)), 1.0, 0.0).astype(BF)

    line = lax.broadcasted_iota(jnp.int32, (experts * SLOTS, rows), 0)
    main = dot(picks(experts * SLOTS, line // SLOTS, line % SLOTS), normed)
    line = lax.broadcasted_iota(jnp.int32, (experts, rows), 0)
    extra = dot(picks(experts, line, jnp.full((experts, rows), SLOTS, jnp.int32)), normed)
    pack(main, extra, spare_ref, (msg_a_ref, msg_b_ref))


def dispatch(hidden, own, own_core, r1, r2, gain, ids_t, experts, earlier):
    rows, width = hidden.shape
    message = jax.ShapeDtypeStruct((experts, width // 256 * SLOTS + 16, 128), BF)
    return pl.pallas_call(
        dispatch_kernel,
        in_specs=[pl.BlockSpec(memory_space=pltpu.VMEM)] * 7
        + [pl.BlockSpec(memory_space=pl.ANY)] * len(earlier),
        out_shape=[jax.ShapeDtypeStruct((rows, width), F32), message, message],
        scratch_shapes=[pltpu.VMEM((experts, 32, 128), F32)],
        compiler_params=pltpu.CompilerParams(vmem_limit_bytes=VMEM),
        cost_estimate=COST,
        name="dispatch",
    )(hidden, own, own_core, r1, r2, gain.reshape(1, width), ids_t, *earlier)


def expert_kernel(n, in_parts, out_parts, *refs):
    msgs, refs = refs[:2], refs[2:]
    w_in, refs = refs[: in_parts * n], refs[in_parts * n :]
    w_out, refs = refs[: out_parts * n], refs[out_parts * n :]
    outs, refs = refs[:2], refs[2:]
    rows_ref, spare_ref, in_buf, out_buf, sems = refs

    def fetch(shard_refs, buf, sem):
        copies, start = [], 0
        for i, ref in enumerate(shard_refs):
            end = start + ref.shape[0]
            copies.append(pltpu.make_async_copy(ref, buf.at[start:end], sems.at[sem + i]))
            copies[-1].start()
            start = end
        return copies

    copies = []
    for s in range(n):
        sem = s * (in_parts + out_parts)
        copies.append(
            (
                fetch(w_in[s * in_parts : (s + 1) * in_parts], in_buf.at[s], sem),
                fetch(w_out[s * out_parts : (s + 1) * out_parts], out_buf.at[s], sem + in_parts),
            )
        )
    unpack(msgs, spare_ref, rows_ref)
    units = out_buf.shape[1]
    total = None
    for s in range(n):
        for copy in copies[s][0]:
            copy.wait()
        joined = dot(rows_ref[...], in_buf[s])
        gate, up = joined[:, :units], joined[:, units:]
        active = (gate / (1.0 + jnp.exp(-gate)) * up).astype(BF)
        for copy in copies[s][1]:
            copy.wait()
        part = dot(active, out_buf[s])
        total = part if total is None else total + part
    experts = outs[0].shape[0]
    main = experts * SLOTS
    pack(total[:main], total[main:], spare_ref, outs)


def run_expert(msgs, w_in, w_out):
    n, in_parts, out_parts = len(w_in), len(w_in[0]), len(w_out[0])
    units = sum(w.shape[0] for w in w_out[0])
    w_in, w_out = sum(w_in, []), sum(w_out, [])
    experts = msgs[0].shape[0]
    width = w_out[0].shape[1]
    rows = experts * (SLOTS + 1)
    return pl.pallas_call(
        functools.partial(expert_kernel, n, in_parts, out_parts),
        in_specs=[pl.BlockSpec(memory_space=pltpu.VMEM)] * 2 + [pl.BlockSpec(memory_space=pl.ANY)] * ((in_parts + out_parts) * n),
        out_specs=[pl.BlockSpec(memory_space=pltpu.VMEM)] * 2,
        out_shape=[jax.ShapeDtypeStruct(m.shape, BF) for m in msgs],
        scratch_shapes=[
            pltpu.VMEM((rows, width), BF),
            pltpu.VMEM((experts, 32, 128), F32),
            pltpu.VMEM((n, width, w_in[0].shape[1]), BF),
            pltpu.VMEM((n, units, width), BF),
            pltpu.SemaphoreType.DMA((n * (in_parts + out_parts),)),
        ],
        compiler_params=pltpu.CompilerParams(vmem_limit_bytes=VMEM),
        cost_estimate=COST,
        name="run_expert",
    )(*msgs, *w_in, *w_out)


def combine_kernel(stream_ref, msg_a_ref, msg_b_ref, ids_ref, gates_ref, out_ref, rows_ref, spare_ref):
    rows = stream_ref.shape[0]
    experts = msg_a_ref.shape[0]
    main = experts * SLOTS
    rows_ref[main:, :] = jnp.zeros((128, rows_ref.shape[1]), BF)
    unpack((msg_a_ref, msg_b_ref), spare_ref, rows_ref)
    before = (
        lax.broadcasted_iota(jnp.int32, (rows, rows), 1)
        < lax.broadcasted_iota(jnp.int32, (rows, rows), 0)
    ).astype(BF)
    place = lax.broadcasted_iota(jnp.int32, (rows, main + 128), 1)
    expert = jnp.where(place < main, place // SLOTS, place - main)
    slot = jnp.where(place < main, place % SLOTS, SLOTS)
    first = ids_ref[:, 0:1] == expert
    second = ids_ref[:, 1:2] == expert
    named = jnp.where(first | second, 1.0, 0.0).astype(BF)
    earlier = dot(before, named)
    weight = jnp.where(first, gates_ref[:, 0:1], jnp.where(second, gates_ref[:, 1:2], 0.0))
    weight = jnp.where(earlier == slot.astype(F32), weight, 0.0)
    mix = stream_ref[...]
    for _ in range(3):
        part = weight.astype(BF)
        mix = mix + dot(part, rows_ref[...])
        weight = weight - part.astype(F32)
    out_ref[...] = mix.astype(BF)


def combine(stream, msgs, ids, gates):
    rows, width = stream.shape
    experts = msgs[0].shape[0]
    return pl.pallas_call(
        combine_kernel,
        out_shape=jax.ShapeDtypeStruct((rows, width), BF),
        scratch_shapes=[
            pltpu.VMEM((experts * SLOTS + 128, width), BF),
            pltpu.VMEM((experts, 32, 128), F32),
        ],
        compiler_params=pltpu.CompilerParams(vmem_limit_bytes=VMEM),
        cost_estimate=COST,
        name="combine",
    )(stream, *msgs, ids, gates)


def shards(
    hidden_in,
    query_heads,
    latent_cache,
    prefix_lens,
    latent_up,
    head_out,
    norm_gain,
    expert_ids,
    gate_weights,
    expert_in,
    expert_out,
):
    experts = lax.axis_size("dp")
    group = lax.axis_size("ep")
    chips = group // 2
    place = lax.axis_index("ep")
    chip, core = place // 2, place % 2

    def to_chip(x, target):
        pairs = [(i, 2 * target(i // 2) + i % 2) for i in range(group)]
        return lax.ppermute(x, "ep", pairs)

    def to_core(x):
        return lax.ppermute(x, "ep", [(i, i ^ 1) for i in range(group)])

    pair = lambda x: x ^ 1
    other = lambda x: chips - 1 - x
    cut = 1280
    w_in = [expert_in[0, :cut].reshape(cut, -1), expert_in[0, cut:].reshape(expert_in.shape[1] - cut, -1)]
    w_out = expert_out[0]
    w_in_pair = [to_chip(w_in[0], pair)]
    w_out_pair = to_chip(w_out, pair)
    w_in_core, w_out_core = [to_core(w) for w in w_in], to_core(w_out)

    keys, values = make_keys(latent_cache[0], latent_up, w_in[:1])

    def attend(target, earlier):
        info = jnp.stack([target, core, prefix_lens[0]]).astype(jnp.int32)
        keep, send = attend_block(info, query_heads, keys, values, head_out, earlier)
        return keep, to_core(send)

    def add(*terms):
        return sum(t.astype(F32) for t in terms).astype(BF)

    far = attend(pair(other(chip)), [])
    near = attend(other(chip), [far[0], *w_in_core, w_in_pair[0]])
    far_sum = add(*far)
    far_in = to_chip(far_sum, other)
    side = attend(pair(chip), [near[0], far_sum, w_out_core])
    near_sum = add(*near)
    near_in = to_chip(near_sum, other)
    own = attend(chip, [side[0], near_sum])
    side_in = to_chip(add(*side, far_in), pair)

    late, near_in, side_in = lax.optimization_barrier((w_in[1], near_in, side_in))
    late = to_chip(late, pair)
    w_in_across = to_core(w_in_pair[0])
    stream, *msgs = dispatch(
        hidden_in, *own, near_in, side_in, norm_gain, expert_ids.T, experts, [w_in_across, w_out_pair]
    )
    exchange = lambda m: lax.all_to_all(m, "dp", split_axis=0, concat_axis=0, tiled=True)
    mine = [exchange(m) for m in msgs]
    theirs = [to_chip(m, other) for m in mine]
    theirs[0], mine[1], late, w_out_pair = lax.optimization_barrier((theirs[0], mine[1], late, w_out_pair))
    w_ins = [w_in, w_in_core, [*w_in_pair, late], [w_in_across, to_core(late)]]
    w_outs = [[w] for w in (w_out, w_out_core, w_out_pair, to_core(w_out_pair))]
    theirs_out = run_expert(theirs, w_ins, w_outs)
    mine_out = run_expert(mine, w_ins, w_outs)
    back = [to_chip(m, other) for m in theirs_out]
    home = [exchange(add(a, b)) for a, b in zip(mine_out, back)]
    return combine(stream, home, expert_ids, gate_weights)


def solution(mesh):
    in_specs = (
        P(("dp", "ep"), None),
        P("dp", "ep"),
        P("dp", None, None),
        P("dp"),
        P(None, "ep"),
        P("ep", None),
        P(),
        P(("dp", "ep"), None),
        P(("dp", "ep"), None),
        P("dp", None, None, "ep"),
        P("dp", "ep", None),
    )
    out_specs = P(("dp", "ep"), None)
    return jax.shard_map(shards, mesh=mesh, in_specs=in_specs, out_specs=out_specs, check_vma=False)
```

```python
import functools

import jax
import jax.numpy as jnp
from jax import lax
from jax.experimental import pallas as pl
from jax.experimental.pallas import tpu as pltpu
from jax.sharding import PartitionSpec as P

NOPE = 128
ROPE = 64
VDIM = 128
LAT = 512
PMAX = 512
SLOTS = 16
BF = jnp.bfloat16
F32 = jnp.float32
VMEM = 56 * 1024 * 1024
KEYS_VMEM = 36 * 1024 * 1024
COST = pl.CostEstimate(flops=10000000000, transcendentals=0, bytes_accessed=1_000)


def dot(a, b):
    return jnp.dot(a, b, preferred_element_type=F32)


def keys_kernel(latent_ref, up_ref, *refs):
    keys_ref, values_ref = refs[-2:]
    rows = latent_ref.shape[1]
    lat = latent_ref[:LAT, :].T
    rot = jnp.concatenate([latent_ref[LAT:, :], jnp.zeros((128 - ROPE, rows), BF)], 0).T.astype(F32)
    rot_even, rot_odd = rot.astype(BF), pltpu.roll(rot, 64, 1)
    low = lax.broadcasted_iota(jnp.int32, (rows, 128), 1) < 64
    for head in range(keys_ref.shape[0]):
        unpacked = dot(lat, up_ref[:, head * 256 : (head + 1) * 256])
        values_ref[head] = unpacked[:, 128:].astype(BF)
        if head % 2 == 0:
            keys_ref[head, :, :128] = unpacked[:, :128].astype(BF)
            keys_ref[head, :, 128:] = rot_even
        else:
            turned = pltpu.roll(unpacked[:, :128], 64, 1)
            keys_ref[head, :, :128] = jnp.where(low, 0.0, turned).astype(BF)
            keys_ref[head, :, 128:] = jnp.where(low, turned, rot_odd).astype(BF)


def make_keys(latent_t, up, earlier):
    rows = latent_t.shape[1]
    heads = up.shape[1] // (NOPE + VDIM)
    made = pl.pallas_call(
        keys_kernel,
        in_specs=[pl.BlockSpec(memory_space=pltpu.VMEM)] * 2
        + [pl.BlockSpec(memory_space=pl.ANY)] * len(earlier),
        out_specs=[pl.BlockSpec(memory_space=pltpu.VMEM)] * 2,
        out_shape=[
            pltpu.VMEM((heads, rows, 256), BF),
            pltpu.VMEM((heads, rows, 128), BF),
        ],
        compiler_params=pltpu.CompilerParams(vmem_limit_bytes=KEYS_VMEM),
        cost_estimate=COST,
        name="make_keys",
    )(latent_t, up, *earlier)
    return [pltpu.with_memory_space_constraint(m, pltpu.VMEM) for m in made]


def attend_kernel(info_ref, q_hbm_ref, w_hbm_ref, keys_ref, values_ref, *refs):
    keep_ref, send_ref, q_ref, w_ref, heads_ref, sems = refs[-6:]
    pairs, qb = heads_ref.shape[:2]
    half = qb // 2
    block = info_ref[0]
    core = info_ref[1]
    prefix_len = info_ref[2]
    factor = (NOPE + ROPE) ** (-0.5) * 1.4426950408889634
    ones = jnp.ones((qb, 128), BF)
    fetches = []
    for i, part in enumerate((core, 1 - core)):
        rows = pl.ds(pl.multiple_of(block * qb + part * half, half), half)
        fetches.append(
            pltpu.make_async_copy(q_hbm_ref.at[rows, :], q_ref.at[i * half : (i + 1) * half, :], sems.at[i])
        )
    fetches.append(pltpu.make_async_copy(w_hbm_ref, w_ref, sems.at[2]))
    for fetch in fetches:
        fetch.start()
    for fetch in fetches[:2]:
        fetch.wait()
    prefix_col = lax.broadcasted_iota(jnp.int32, (1, PMAX), 1)
    bias = jnp.where(prefix_col < prefix_len, 0.0, -1e30)

    def one_head(pair, h, count):
        q = q_ref[:, pl.ds(pl.multiple_of(pair * 384 + h * 128, 128), 256)]
        head = pair * 2 + h
        scores = []
        for t in range(PMAX // qb + count):
            s = lax.dot_general(
                q,
                keys_ref[head, t * qb : (t + 1) * qb, :],
                (((1,), (1,)), ((), ())),
                preferred_element_type=F32,
            )
            if t < PMAX // qb:
                s = s + bias[:, t * qb : (t + 1) * qb]
            elif t == PMAX // qb + count - 1:
                col = lax.broadcasted_iota(jnp.int32, (qb, qb), 1)
                row = lax.broadcasted_iota(jnp.int32, (qb, qb), 0)
                s = jnp.where(col <= (row + core * half) % qb, s, -1e30)
            scores.append(s)
        peak = functools.reduce(jnp.maximum, scores)
        peak = jnp.max(peak, 1, keepdims=True)
        total = jnp.zeros((qb, 256), F32)
        for t, s in enumerate(scores):
            p = jnp.exp2((s - peak) * factor).astype(BF)
            v = values_ref[head, t * qb : (t + 1) * qb, :]
            total = total + dot(p, jnp.concatenate([v, ones], 1))
        return (total[:, :128] / total[:, 128:]).astype(BF)

    for b in range(4):

        @pl.when(block == b)
        def _(b=b):
            @pl.loop(0, pairs)
            def _(pair):
                heads_ref[pair, :, :128] = one_head(pair, 0, b + 1)
                heads_ref[pair, :, 128:] = one_head(pair, 1, b + 1)

    attended = jnp.concatenate([heads_ref[i] for i in range(pairs)], 1)
    fetches[2].wait()
    out = dot(attended, w_ref[...])
    keep_ref[...] = out[:half].astype(BF)
    send_ref[...] = out[half:].astype(BF)


def attend_block(info, queries, out_w, made, earlier):
    queries, out_w = [pltpu.with_memory_space_constraint(x, pltpu.HBM) for x in (queries, out_w)]
    heads = made[0].shape[0]
    width = out_w.shape[1]
    qb = 256
    return pl.pallas_call(
        attend_kernel,
        in_specs=[pl.BlockSpec(memory_space=pltpu.SMEM)]
        + [pl.BlockSpec(memory_space=pl.ANY)] * 2
        + [pl.BlockSpec(memory_space=pltpu.VMEM)] * 2
        + [pl.BlockSpec(memory_space=pl.ANY)] * len(earlier),
        out_specs=[pl.BlockSpec(memory_space=pltpu.VMEM)] * 2,
        out_shape=[jax.ShapeDtypeStruct((qb // 2, width), BF)] * 2,
        scratch_shapes=[
            pltpu.VMEM((qb, queries.shape[1]), BF),
            pltpu.VMEM(out_w.shape, BF),
            pltpu.VMEM((heads // 2, qb, 256), BF),
            pltpu.SemaphoreType.DMA((3,)),
        ],
        compiler_params=pltpu.CompilerParams(vmem_limit_bytes=KEYS_VMEM),
        cost_estimate=COST,
        name="attend_block",
    )(info, queries, out_w, *made, *earlier)


def pack(main, extra, spare_ref, msg_refs):
    experts = msg_refs[0].shape[0]
    spare_ref[...] = jnp.zeros_like(spare_ref)
    per = main.shape[1] // 128 // len(msg_refs)
    for i, msg in enumerate(msg_refs):
        for c in range(per):
            lanes = slice((i * per + c) * 128, (i * per + c + 1) * 128)
            msg[:, c * SLOTS : (c + 1) * SLOTS, :] = (
                main[:, lanes].astype(BF).reshape(experts, SLOTS, 128)
            )
            spare_ref[:, i * 16 + c, :] = extra[:, lanes].astype(F32)
        msg[:, per * SLOTS :, :] = spare_ref[:, i * 16 : (i + 1) * 16, :].astype(BF)


def unpack(msg_refs, spare_ref, rows_ref):
    experts = msg_refs[0].shape[0]
    main = experts * SLOTS
    per = rows_ref.shape[1] // 128 // len(msg_refs)
    for i, msg in enumerate(msg_refs):
        spare_ref[:, i * 16 : (i + 1) * 16, :] = msg[:, per * SLOTS :, :].astype(F32)
        for c in range(per):
            lanes = slice((i * per + c) * 128, (i * per + c + 1) * 128)
            rows_ref[:main, lanes] = msg[:, c * SLOTS : (c + 1) * SLOTS, :].reshape(main, 128)
            rows_ref[main : main + experts, lanes] = spare_ref[:, i * 16 + c, :].astype(BF)


def dispatch_kernel(
    hidden_ref, own_ref, own_core_ref, r1_ref, r2_ref, gain_ref, ids_ref, *refs
):
    stream_ref, msg_a_ref, msg_b_ref, spare_ref = refs[-4:]
    rows = hidden_ref.shape[0]
    experts = msg_a_ref.shape[0]
    stream = hidden_ref[...].astype(F32)
    for ref in (own_ref, own_core_ref, r1_ref, r2_ref):
        stream = stream + ref[...].astype(F32)
    stream_ref[...] = stream
    mean = jnp.mean(stream * stream, -1, keepdims=True)
    normed = (stream * lax.rsqrt(mean + 1e-6) * gain_ref[...]).astype(BF)
    before = (
        lax.broadcasted_iota(jnp.int32, (rows, rows), 0)
        < lax.broadcasted_iota(jnp.int32, (rows, rows), 1)
    ).astype(BF)

    def picks(count, expert, slot):
        named = (ids_ref[0:1, :] == expert) | (ids_ref[1:2, :] == expert)
        earlier = dot(named.astype(F32).astype(BF), before)
        return jnp.where(named & (earlier == slot.astype(F32)), 1.0, 0.0).astype(BF)

    line = lax.broadcasted_iota(jnp.int32, (experts * SLOTS, rows), 0)
    main = dot(picks(experts * SLOTS, line // SLOTS, line % SLOTS), normed)
    line = lax.broadcasted_iota(jnp.int32, (experts, rows), 0)
    extra = dot(picks(experts, line, jnp.full((experts, rows), SLOTS, jnp.int32)), normed)
    pack(main, extra, spare_ref, (msg_a_ref, msg_b_ref))


def dispatch(hidden, own, own_core, r1, r2, gain, ids_t, experts, earlier):
    rows, width = hidden.shape
    message = jax.ShapeDtypeStruct((experts, width // 256 * SLOTS + 16, 128), BF)
    return pl.pallas_call(
        dispatch_kernel,
        in_specs=[pl.BlockSpec(memory_space=pltpu.VMEM)] * 7
        + [pl.BlockSpec(memory_space=pl.ANY)] * len(earlier),
        out_shape=[jax.ShapeDtypeStruct((rows, width), F32), message, message],
        scratch_shapes=[pltpu.VMEM((experts, 32, 128), F32)],
        compiler_params=pltpu.CompilerParams(vmem_limit_bytes=VMEM),
        cost_estimate=COST,
        name="dispatch",
    )(hidden, own, own_core, r1, r2, gain.reshape(1, width), ids_t, *earlier)


def expert_kernel(n, *refs):
    msgs, refs = refs[:2], refs[2:]
    shards, refs = refs[: 2 * n], refs[2 * n :]
    outs, refs = refs[:2], refs[2:]
    rows_ref, spare_ref, in_buf, out_buf, sems = refs
    cut, width = shards[0].shape
    rest = in_buf.shape[1] - cut
    units = out_buf.shape[1]
    copies = []
    for s in range(n):
        first, second = shards[2 * s : 2 * s + 2]
        places = [(first, in_buf.at[s, :cut]), (second.at[:rest], in_buf.at[s, cut:])]
        for i in range(out_buf.shape[2] // width):
            block = second.at[rest + i * units : rest + (i + 1) * units]
            places.append((block, out_buf.at[s, :, i * width : (i + 1) * width]))
        copies.append([pltpu.make_async_copy(*p, sems.at[s, i]) for i, p in enumerate(places)])
        for copy in copies[-1]:
            copy.start()
    unpack(msgs, spare_ref, rows_ref)
    total = None
    for s in range(n):
        for copy in copies[s][:2]:
            copy.wait()
        joined = dot(rows_ref[...], in_buf[s])
        gate, up = joined[:, :units], joined[:, units:]
        active = (gate / (1.0 + jnp.exp(-gate)) * up).astype(BF)
        for copy in copies[s][2:]:
            copy.wait()
        part = dot(active, out_buf[s])
        total = part if total is None else total + part
    experts = outs[0].shape[0]
    main = experts * SLOTS
    pack(total[:main], total[main:], spare_ref, outs)


def run_expert(msgs, shards, depth):
    n = len(shards)
    experts = msgs[0].shape[0]
    cols = shards[0][0].shape[1]
    units = cols // 2
    rows = experts * (SLOTS + 1)
    return pl.pallas_call(
        functools.partial(expert_kernel, n),
        in_specs=[pl.BlockSpec(memory_space=pltpu.VMEM)] * 2 + [pl.BlockSpec(memory_space=pl.ANY)] * (2 * n),
        out_specs=[pl.BlockSpec(memory_space=pltpu.VMEM)] * 2,
        out_shape=[jax.ShapeDtypeStruct(m.shape, BF) for m in msgs],
        scratch_shapes=[
            pltpu.VMEM((rows, depth), BF),
            pltpu.VMEM((experts, 32, 128), F32),
            pltpu.VMEM((n, depth, cols), BF),
            pltpu.VMEM((n, units, depth), BF),
            pltpu.SemaphoreType.DMA((n, 2 + depth // cols)),
        ],
        compiler_params=pltpu.CompilerParams(vmem_limit_bytes=VMEM),
        cost_estimate=COST,
        name="run_expert",
    )(*msgs, *sum(shards, []))


def combine_kernel(stream_ref, msg_a_ref, msg_b_ref, ids_ref, gates_ref, out_ref, rows_ref, spare_ref):
    rows = stream_ref.shape[0]
    experts = msg_a_ref.shape[0]
    main = experts * SLOTS
    rows_ref[main:, :] = jnp.zeros((128, rows_ref.shape[1]), BF)
    unpack((msg_a_ref, msg_b_ref), spare_ref, rows_ref)
    before = (
        lax.broadcasted_iota(jnp.int32, (rows, rows), 1)
        < lax.broadcasted_iota(jnp.int32, (rows, rows), 0)
    ).astype(BF)
    place = lax.broadcasted_iota(jnp.int32, (rows, main + 128), 1)
    expert = jnp.where(place < main, place // SLOTS, place - main)
    slot = jnp.where(place < main, place % SLOTS, SLOTS)
    first = ids_ref[:, 0:1] == expert
    second = ids_ref[:, 1:2] == expert
    named = jnp.where(first | second, 1.0, 0.0).astype(BF)
    earlier = dot(before, named)
    weight = jnp.where(first, gates_ref[:, 0:1], jnp.where(second, gates_ref[:, 1:2], 0.0))
    weight = jnp.where(earlier == slot.astype(F32), weight, 0.0)
    mix = stream_ref[...]
    for _ in range(3):
        part = weight.astype(BF)
        mix = mix + dot(part, rows_ref[...])
        weight = weight - part.astype(F32)
    out_ref[...] = mix.astype(BF)


def combine(stream, msgs, ids, gates):
    rows, width = stream.shape
    experts = msgs[0].shape[0]
    return pl.pallas_call(
        combine_kernel,
        out_shape=jax.ShapeDtypeStruct((rows, width), BF),
        scratch_shapes=[
            pltpu.VMEM((experts * SLOTS + 128, width), BF),
            pltpu.VMEM((experts, 32, 128), F32),
        ],
        compiler_params=pltpu.CompilerParams(vmem_limit_bytes=VMEM),
        cost_estimate=COST,
        name="combine",
    )(stream, *msgs, ids, gates)


def shards(
    hidden_in,
    query_heads,
    latent_cache,
    prefix_lens,
    latent_up,
    head_out,
    norm_gain,
    expert_ids,
    gate_weights,
    expert_in,
    expert_out,
):
    experts = lax.axis_size("dp")
    group = lax.axis_size("ep")
    chips = group // 2
    place = lax.axis_index("ep")
    chip, core = place // 2, place % 2

    def to_chip(x, target):
        pairs = [(i, 2 * target(i // 2) + i % 2) for i in range(group)]
        return lax.ppermute(x, "ep", pairs)

    def to_core(x):
        return lax.ppermute(x, "ep", [(i, i ^ 1) for i in range(group)])

    pair = lambda x: x ^ 1
    other = lambda x: chips - 1 - x
    depth = expert_in.shape[1]
    cut = 2304
    first = expert_in[0, :cut].reshape(cut, -1)
    first_pair, first_core = to_chip(first, pair), to_core(first)

    made = make_keys(latent_cache[0].T, latent_up, [first])

    def attend(target, earlier):
        info = jnp.stack([target, core, prefix_lens[0]]).astype(jnp.int32)
        keep, send = attend_block(info, query_heads, head_out, made, earlier)
        return keep, to_core(send)

    def add(*terms):
        return sum(t.astype(F32) for t in terms).astype(BF)

    far = attend(pair(other(chip)), [])
    far_sum = add(*far)
    near = attend(other(chip), [far[0]])
    far_in = to_chip(far_sum, other)
    side = attend(pair(chip), [near[0], far_sum])
    near_sum = add(*near)
    near_in = to_chip(near_sum, other)
    own = attend(chip, [side[0], near_sum, first_pair])
    side_in = to_chip(add(*side, far_in), pair)

    rest_in, rest_out, _ = lax.optimization_barrier((expert_in[0, cut:], expert_out[0], own[0]))
    cols = first.shape[1]
    second = [rest_in.reshape(depth - cut, cols)]
    second = jnp.concatenate(second + [rest_out[:, i : i + cols] for i in range(0, depth, cols)], 0)
    second, near_in, side_in = lax.optimization_barrier((second, near_in, side_in))
    second_pair, second_core = to_chip(second, pair), to_core(second)
    first_across = to_core(first_pair)
    stream, *msgs = dispatch(
        hidden_in, *own, near_in, side_in, norm_gain, expert_ids.T, experts, [first_across, first_core]
    )
    exchange = lambda m: lax.all_to_all(m, "dp", split_axis=0, concat_axis=0, tiled=True)
    mine = [exchange(m) for m in msgs]
    theirs = [to_chip(m, other) for m in mine]
    *theirs, second_pair, second_core = lax.optimization_barrier((*theirs, second_pair, second_core))
    weights = [[first, second], [first_core, second_core]]
    weights += [[first_pair, second_pair], [first_across, to_core(second_pair)]]
    theirs_out = run_expert(theirs, weights, depth)
    mine_out = run_expert(mine, weights, depth)
    back = [to_chip(m, other) for m in theirs_out]
    home = [exchange(add(a, b)) for a, b in zip(mine_out, back)]
    return combine(stream, home, expert_ids, gate_weights)


def solution(mesh):
    in_specs = (
        P(("dp", "ep"), None),
        P("dp", "ep"),
        P("dp", None, None),
        P("dp"),
        P(None, "ep"),
        P("ep", None),
        P(),
        P(("dp", "ep"), None),
        P(("dp", "ep"), None),
        P("dp", None, None, "ep"),
        P("dp", "ep", None),
    )
    out_specs = P(("dp", "ep"), None)
    return jax.shard_map(shards, mesh=mesh, in_specs=in_specs, out_specs=out_specs, check_vma=False)
```

```python
import functools

import jax
import jax.numpy as jnp
from jax import lax
from jax.experimental import pallas as pl
from jax.experimental.pallas import tpu as pltpu
from jax.sharding import PartitionSpec as P

NOPE = 128
ROPE = 64
VDIM = 128
LAT = 512
PMAX = 512
SLOTS = 16
BF = jnp.bfloat16
F32 = jnp.float32
VMEM = 56 * 1024 * 1024
KEYS_VMEM = 36 * 1024 * 1024
COST = pl.CostEstimate(flops=10000000000, transcendentals=0, bytes_accessed=1_000)


def dot(a, b):
    return jnp.dot(a, b, preferred_element_type=F32)


def keys_kernel(latent_ref, up_ref, *refs):
    keys_ref, values_ref = refs[-2:]
    rows = latent_ref.shape[1]
    lat = latent_ref[:LAT, :].T
    rot = jnp.concatenate([latent_ref[LAT:, :], jnp.zeros((128 - ROPE, rows), BF)], 0).T.astype(F32)
    rot_even, rot_odd = rot.astype(BF), pltpu.roll(rot, 64, 1)
    low = lax.broadcasted_iota(jnp.int32, (rows, 128), 1) < 64
    for head in range(keys_ref.shape[0]):
        unpacked = dot(lat, up_ref[:, head * 256 : (head + 1) * 256])
        values_ref[head] = unpacked[:, 128:].astype(BF)
        if head % 2 == 0:
            keys_ref[head, :, :128] = unpacked[:, :128].astype(BF)
            keys_ref[head, :, 128:] = rot_even
        else:
            turned = pltpu.roll(unpacked[:, :128], 64, 1)
            keys_ref[head, :, :128] = jnp.where(low, 0.0, turned).astype(BF)
            keys_ref[head, :, 128:] = jnp.where(low, turned, rot_odd).astype(BF)


def make_keys(latent_t, up, earlier):
    rows = latent_t.shape[1]
    heads = up.shape[1] // (NOPE + VDIM)
    made = pl.pallas_call(
        keys_kernel,
        in_specs=[pl.BlockSpec(memory_space=pltpu.VMEM)] * 2
        + [pl.BlockSpec(memory_space=pl.ANY)] * len(earlier),
        out_specs=[pl.BlockSpec(memory_space=pltpu.VMEM)] * 2,
        out_shape=[
            pltpu.VMEM((heads, rows, 256), BF),
            pltpu.VMEM((heads, rows, 128), BF),
        ],
        compiler_params=pltpu.CompilerParams(vmem_limit_bytes=KEYS_VMEM),
        cost_estimate=COST,
        name="make_keys",
    )(latent_t, up, *earlier)
    return [pltpu.with_memory_space_constraint(m, pltpu.VMEM) for m in made]


def attend_kernel(info_ref, q_hbm_ref, w_hbm_ref, keys_ref, values_ref, *refs):
    keep_ref, send_ref, q_ref, w_ref, heads_ref, sems = refs[-6:]
    pairs, qb = heads_ref.shape[:2]
    half = qb // 2
    block = info_ref[0]
    core = info_ref[1]
    prefix_len = info_ref[2]
    factor = (NOPE + ROPE) ** (-0.5) * 1.4426950408889634
    ones = jnp.ones((qb, 128), BF)
    fetches = []
    for i, part in enumerate((core, 1 - core)):
        rows = pl.ds(pl.multiple_of(block * qb + part * half, half), half)
        fetches.append(
            pltpu.make_async_copy(q_hbm_ref.at[rows, :], q_ref.at[i * half : (i + 1) * half, :], sems.at[i])
        )
    fetches.append(pltpu.make_async_copy(w_hbm_ref, w_ref, sems.at[2]))
    for fetch in fetches:
        fetch.start()
    for fetch in fetches[:2]:
        fetch.wait()
    prefix_col = lax.broadcasted_iota(jnp.int32, (1, PMAX), 1)
    bias = jnp.where(prefix_col < prefix_len, 0.0, -1e30)

    def one_head(pair, h, count):
        q = q_ref[:, pl.ds(pl.multiple_of(pair * 384 + h * 128, 128), 256)]
        head = pair * 2 + h
        scores = []
        for t in range(PMAX // qb + count):
            s = lax.dot_general(
                q,
                keys_ref[head, t * qb : (t + 1) * qb, :],
                (((1,), (1,)), ((), ())),
                preferred_element_type=F32,
            )
            if t < PMAX // qb:
                s = s + bias[:, t * qb : (t + 1) * qb]
            elif t == PMAX // qb + count - 1:
                col = lax.broadcasted_iota(jnp.int32, (qb, qb), 1)
                row = lax.broadcasted_iota(jnp.int32, (qb, qb), 0)
                s = jnp.where(col <= (row + core * half) % qb, s, -1e30)
            scores.append(s)
        peak = functools.reduce(jnp.maximum, scores)
        peak = jnp.max(peak, 1, keepdims=True)
        total = jnp.zeros((qb, 256), F32)
        for t, s in enumerate(scores):
            p = jnp.exp2((s - peak) * factor).astype(BF)
            v = values_ref[head, t * qb : (t + 1) * qb, :]
            total = total + dot(p, jnp.concatenate([v, ones], 1))
        return (total[:, :128] / total[:, 128:]).astype(BF)

    for b in range(4):

        @pl.when(block == b)
        def _(b=b):
            @pl.loop(0, pairs)
            def _(pair):
                heads_ref[pair, :, :128] = one_head(pair, 0, b + 1)
                heads_ref[pair, :, 128:] = one_head(pair, 1, b + 1)

    attended = jnp.concatenate([heads_ref[i] for i in range(pairs)], 1)
    fetches[2].wait()
    out = dot(attended, w_ref[...])
    keep_ref[...] = out[:half].astype(BF)
    send_ref[...] = out[half:].astype(BF)


def attend_block(info, queries, out_w, made, earlier):
    queries, out_w = [pltpu.with_memory_space_constraint(x, pltpu.HBM) for x in (queries, out_w)]
    heads = made[0].shape[0]
    width = out_w.shape[1]
    qb = 256
    return pl.pallas_call(
        attend_kernel,
        in_specs=[pl.BlockSpec(memory_space=pltpu.SMEM)]
        + [pl.BlockSpec(memory_space=pl.ANY)] * 2
        + [pl.BlockSpec(memory_space=pltpu.VMEM)] * 2
        + [pl.BlockSpec(memory_space=pl.ANY)] * len(earlier),
        out_specs=[pl.BlockSpec(memory_space=pltpu.VMEM)] * 2,
        out_shape=[jax.ShapeDtypeStruct((qb // 2, width), BF)] * 2,
        scratch_shapes=[
            pltpu.VMEM((qb, queries.shape[1]), BF),
            pltpu.VMEM(out_w.shape, BF),
            pltpu.VMEM((heads // 2, qb, 256), BF),
            pltpu.SemaphoreType.DMA((3,)),
        ],
        compiler_params=pltpu.CompilerParams(vmem_limit_bytes=KEYS_VMEM),
        cost_estimate=COST,
        name="attend_block",
    )(info, queries, out_w, *made, *earlier)


def pack(main, extra, spare_ref, msg_refs):
    experts = msg_refs[0].shape[0]
    spare_ref[...] = jnp.zeros_like(spare_ref)
    per = main.shape[1] // 128 // len(msg_refs)
    for i, msg in enumerate(msg_refs):
        for c in range(per):
            lanes = slice((i * per + c) * 128, (i * per + c + 1) * 128)
            msg[:, c * SLOTS : (c + 1) * SLOTS, :] = (
                main[:, lanes].astype(BF).reshape(experts, SLOTS, 128)
            )
            spare_ref[:, i * 16 + c, :] = extra[:, lanes].astype(F32)
        msg[:, per * SLOTS :, :] = spare_ref[:, i * 16 : (i + 1) * 16, :].astype(BF)


def unpack(msg_refs, spare_ref, rows_ref):
    experts = msg_refs[0].shape[0]
    main = experts * SLOTS
    per = rows_ref.shape[1] // 128 // len(msg_refs)
    for i, msg in enumerate(msg_refs):
        spare_ref[:, i * 16 : (i + 1) * 16, :] = msg[:, per * SLOTS :, :].astype(F32)
        for c in range(per):
            lanes = slice((i * per + c) * 128, (i * per + c + 1) * 128)
            rows_ref[:main, lanes] = msg[:, c * SLOTS : (c + 1) * SLOTS, :].reshape(main, 128)
            rows_ref[main : main + experts, lanes] = spare_ref[:, i * 16 + c, :].astype(BF)


def dispatch_kernel(
    hidden_ref, own_ref, own_core_ref, r1_ref, r2_ref, gain_ref, ids_ref, *refs
):
    stream_ref, msg_a_ref, msg_b_ref, spare_ref = refs[-4:]
    rows = hidden_ref.shape[0]
    experts = msg_a_ref.shape[0]
    stream = hidden_ref[...].astype(F32)
    for ref in (own_ref, own_core_ref, r1_ref, r2_ref):
        stream = stream + ref[...].astype(F32)
    stream_ref[...] = stream
    mean = jnp.mean(stream * stream, -1, keepdims=True)
    normed = (stream * lax.rsqrt(mean + 1e-6) * gain_ref[...]).astype(BF)
    before = (
        lax.broadcasted_iota(jnp.int32, (rows, rows), 0)
        < lax.broadcasted_iota(jnp.int32, (rows, rows), 1)
    ).astype(BF)

    def picks(count, expert, slot):
        named = (ids_ref[0:1, :] == expert) | (ids_ref[1:2, :] == expert)
        earlier = dot(named.astype(F32).astype(BF), before)
        return jnp.where(named & (earlier == slot.astype(F32)), 1.0, 0.0).astype(BF)

    line = lax.broadcasted_iota(jnp.int32, (experts * SLOTS, rows), 0)
    main = dot(picks(experts * SLOTS, line // SLOTS, line % SLOTS), normed)
    line = lax.broadcasted_iota(jnp.int32, (experts, rows), 0)
    extra = dot(picks(experts, line, jnp.full((experts, rows), SLOTS, jnp.int32)), normed)
    pack(main, extra, spare_ref, (msg_a_ref, msg_b_ref))


def dispatch(hidden, own, own_core, r1, r2, gain, ids_t, experts, earlier):
    rows, width = hidden.shape
    message = jax.ShapeDtypeStruct((experts, width // 256 * SLOTS + 16, 128), BF)
    return pl.pallas_call(
        dispatch_kernel,
        in_specs=[pl.BlockSpec(memory_space=pltpu.VMEM)] * 7
        + [pl.BlockSpec(memory_space=pl.ANY)] * len(earlier),
        out_shape=[jax.ShapeDtypeStruct((rows, width), F32), message, message],
        scratch_shapes=[pltpu.VMEM((experts, 32, 128), F32)],
        compiler_params=pltpu.CompilerParams(vmem_limit_bytes=VMEM),
        cost_estimate=COST,
        name="dispatch",
    )(hidden, own, own_core, r1, r2, gain.reshape(1, width), ids_t, *earlier)


def expert_kernel(counts, *refs):
    n = len(counts)
    msgs, refs = refs[:2], refs[2:]
    shards = []
    for count in counts:
        shards.append(refs[:count])
        refs = refs[count:]
    outs, refs = refs[:2], refs[2:]
    rows_ref, spare_ref, in_buf, out_buf, sems = refs
    cut, width = shards[0][0].shape
    rest = in_buf.shape[1] - cut
    units = out_buf.shape[1]
    copies = []
    for s in range(n):
        places = [(shards[s][0], in_buf.at[s, :cut])]
        start = 0
        for piece in shards[s][1:]:
            for row in range(start, start + piece.shape[0], units):
                src = piece.at[row - start : row - start + units]
                if row < rest:
                    dst = in_buf.at[s, cut + row : cut + row + units]
                else:
                    col = (row - rest) // units * width
                    dst = out_buf.at[s, :, col : col + width]
                places.append((src, dst))
            start += piece.shape[0]
        copies.append([pltpu.make_async_copy(*p, sems.at[s, i]) for i, p in enumerate(places)])
        for copy in copies[-1]:
            copy.start()
    unpack(msgs, spare_ref, rows_ref)
    total = None
    ready = 1 + rest // units
    for s in range(n):
        for copy in copies[s][:ready]:
            copy.wait()
        joined = dot(rows_ref[...], in_buf[s])
        gate, up = joined[:, :units], joined[:, units:]
        active = (gate / (1.0 + jnp.exp(-gate)) * up).astype(BF)
        for copy in copies[s][ready:]:
            copy.wait()
        part = dot(active, out_buf[s])
        total = part if total is None else total + part
    experts = outs[0].shape[0]
    main = experts * SLOTS
    pack(total[:main], total[main:], spare_ref, outs)


def run_expert(msgs, shards, depth):
    n = len(shards)
    counts = [len(shard) for shard in shards]
    experts = msgs[0].shape[0]
    cols = shards[0][0].shape[1]
    units = cols // 2
    rows = experts * (SLOTS + 1)
    return pl.pallas_call(
        functools.partial(expert_kernel, counts),
        in_specs=[pl.BlockSpec(memory_space=pltpu.VMEM)] * 2 + [pl.BlockSpec(memory_space=pl.ANY)] * sum(counts),
        out_specs=[pl.BlockSpec(memory_space=pltpu.VMEM)] * 2,
        out_shape=[jax.ShapeDtypeStruct(m.shape, BF) for m in msgs],
        scratch_shapes=[
            pltpu.VMEM((rows, depth), BF),
            pltpu.VMEM((experts, 32, 128), F32),
            pltpu.VMEM((n, depth, cols), BF),
            pltpu.VMEM((n, units, depth), BF),
            pltpu.SemaphoreType.DMA((n, 1 + (depth - shards[0][0].shape[0]) // units + depth // cols)),
        ],
        compiler_params=pltpu.CompilerParams(vmem_limit_bytes=VMEM),
        cost_estimate=COST,
        name="run_expert",
    )(*msgs, *sum(shards, []))


def combine_kernel(stream_ref, msg_a_ref, msg_b_ref, ids_ref, gates_ref, out_ref, rows_ref, spare_ref):
    rows = stream_ref.shape[0]
    experts = msg_a_ref.shape[0]
    main = experts * SLOTS
    rows_ref[main:, :] = jnp.zeros((128, rows_ref.shape[1]), BF)
    unpack((msg_a_ref, msg_b_ref), spare_ref, rows_ref)
    before = (
        lax.broadcasted_iota(jnp.int32, (rows, rows), 1)
        < lax.broadcasted_iota(jnp.int32, (rows, rows), 0)
    ).astype(BF)
    place = lax.broadcasted_iota(jnp.int32, (rows, main + 128), 1)
    expert = jnp.where(place < main, place // SLOTS, place - main)
    slot = jnp.where(place < main, place % SLOTS, SLOTS)
    first = ids_ref[:, 0:1] == expert
    second = ids_ref[:, 1:2] == expert
    named = jnp.where(first | second, 1.0, 0.0).astype(BF)
    earlier = dot(before, named)
    weight = jnp.where(first, gates_ref[:, 0:1], jnp.where(second, gates_ref[:, 1:2], 0.0))
    weight = jnp.where(earlier == slot.astype(F32), weight, 0.0)
    mix = stream_ref[...]
    for _ in range(3):
        part = weight.astype(BF)
        mix = mix + dot(part, rows_ref[...])
        weight = weight - part.astype(F32)
    out_ref[...] = mix.astype(BF)


def combine(stream, msgs, ids, gates):
    rows, width = stream.shape
    experts = msgs[0].shape[0]
    return pl.pallas_call(
        combine_kernel,
        out_shape=jax.ShapeDtypeStruct((rows, width), BF),
        scratch_shapes=[
            pltpu.VMEM((experts * SLOTS + 128, width), BF),
            pltpu.VMEM((experts, 32, 128), F32),
        ],
        compiler_params=pltpu.CompilerParams(vmem_limit_bytes=VMEM),
        cost_estimate=COST,
        name="combine",
    )(stream, *msgs, ids, gates)


def shards(
    hidden_in,
    query_heads,
    latent_cache,
    prefix_lens,
    latent_up,
    head_out,
    norm_gain,
    expert_ids,
    gate_weights,
    expert_in,
    expert_out,
):
    experts = lax.axis_size("dp")
    group = lax.axis_size("ep")
    chips = group // 2
    place = lax.axis_index("ep")
    chip, core = place // 2, place % 2

    def to_chip(x, target):
        pairs = [(i, 2 * target(i // 2) + i % 2) for i in range(group)]
        return lax.ppermute(x, "ep", pairs)

    def to_core(x):
        return lax.ppermute(x, "ep", [(i, i ^ 1) for i in range(group)])

    pair = lambda x: x ^ 1
    other = lambda x: chips - 1 - x
    depth = expert_in.shape[1]
    cut = 2304
    first = expert_in[0, :cut].reshape(cut, -1)
    first_pair, first_core = to_chip(first, pair), to_core(first)

    made = make_keys(latent_cache[0].T, latent_up, [first])

    def attend(target, earlier):
        info = jnp.stack([target, core, prefix_lens[0]]).astype(jnp.int32)
        keep, send = attend_block(info, query_heads, head_out, made, earlier)
        return keep, to_core(send)

    def add(*terms):
        return sum(t.astype(F32) for t in terms).astype(BF)

    far = attend(pair(other(chip)), [])
    far_sum = add(*far)
    near = attend(other(chip), [far[0]])
    far_in = to_chip(far_sum, other)
    side = attend(pair(chip), [near[0], far_sum])
    near_sum = add(*near)
    near_in = to_chip(near_sum, other)
    own = attend(chip, [side[0], near_sum, first_pair])
    side_in = to_chip(add(*side, far_in), pair)

    rest_in, rest_out, _ = lax.optimization_barrier((expert_in[0, cut:], expert_out[0], own[0]))
    cols = first.shape[1]
    second = [rest_in.reshape(depth - cut, cols)]
    second = jnp.concatenate(second + [rest_out[:, i : i + cols] for i in range(0, depth, cols)], 0)
    second, near_in, side_in = lax.optimization_barrier((second, near_in, side_in))
    second_pair, second_core = to_chip(second, pair), to_core(second)
    first_across = to_core(first_pair)
    stream, *msgs = dispatch(
        hidden_in, *own, near_in, side_in, norm_gain, expert_ids.T, experts, [first_across, first_core]
    )
    exchange = lambda m: lax.all_to_all(m, "dp", split_axis=0, concat_axis=0, tiled=True)
    mine = [exchange(m) for m in msgs]
    theirs = [to_chip(m, other) for m in mine]
    theirs[0], mine[1], second_pair, second_core = lax.optimization_barrier(
        (theirs[0], mine[1], second_pair, second_core)
    )
    step = second_pair.shape[0] // 4
    second_across = [to_core(second_pair[i : i + step]) for i in range(0, 4 * step, step)]
    weights = [[first, second], [first_core, second_core]]
    weights += [[first_pair, second_pair], [first_across, *second_across]]
    theirs_out = run_expert(theirs, weights, depth)
    mine_out = run_expert(mine, weights, depth)
    back = [to_chip(m, other) for m in theirs_out]
    home = [exchange(add(a, b)) for a, b in zip(mine_out, back)]
    return combine(stream, home, expert_ids, gate_weights)


def solution(mesh):
    in_specs = (
        P(("dp", "ep"), None),
        P("dp", "ep"),
        P("dp", None, None),
        P("dp"),
        P(None, "ep"),
        P("ep", None),
        P(),
        P(("dp", "ep"), None),
        P(("dp", "ep"), None),
        P("dp", None, None, "ep"),
        P("dp", "ep", None),
    )
    out_specs = P(("dp", "ep"), None)
    return jax.shard_map(shards, mesh=mesh, in_specs=in_specs, out_specs=out_specs, check_vma=False)
```

```python
import functools

import jax
import jax.numpy as jnp
from jax import lax
from jax.experimental import pallas as pl
from jax.experimental.pallas import tpu as pltpu
from jax.sharding import PartitionSpec as P

NOPE = 128
ROPE = 64
VDIM = 128
LAT = 512
PMAX = 512
SLOTS = 16
BF = jnp.bfloat16
F32 = jnp.float32
VMEM = 56 * 1024 * 1024
KEYS_VMEM = 36 * 1024 * 1024
COST = pl.CostEstimate(flops=10000000000, transcendentals=0, bytes_accessed=1_000)


def dot(a, b):
    return jnp.dot(a, b, preferred_element_type=F32)


def keys_kernel(latent_ref, up_ref, *refs):
    keys_ref, values_ref = refs[-2:]
    rows = latent_ref.shape[1]
    lat = latent_ref[:LAT, :].T
    rot = jnp.concatenate([latent_ref[LAT:, :], jnp.zeros((128 - ROPE, rows), BF)], 0).T.astype(F32)
    rot_even, rot_odd = rot.astype(BF), pltpu.roll(rot, 64, 1)
    low = lax.broadcasted_iota(jnp.int32, (rows, 128), 1) < 64
    for head in range(keys_ref.shape[0]):
        unpacked = dot(lat, up_ref[:, head * 256 : (head + 1) * 256])
        values_ref[head] = unpacked[:, 128:].astype(BF)
        if head % 2 == 0:
            keys_ref[head, :, :128] = unpacked[:, :128].astype(BF)
            keys_ref[head, :, 128:] = rot_even
        else:
            turned = pltpu.roll(unpacked[:, :128], 64, 1)
            keys_ref[head, :, :128] = jnp.where(low, 0.0, turned).astype(BF)
            keys_ref[head, :, 128:] = jnp.where(low, turned, rot_odd).astype(BF)


def make_keys(latent_t, up, earlier):
    rows = latent_t.shape[1]
    heads = up.shape[1] // (NOPE + VDIM)
    made = pl.pallas_call(
        keys_kernel,
        in_specs=[pl.BlockSpec(memory_space=pltpu.VMEM)] * 2
        + [pl.BlockSpec(memory_space=pl.ANY)] * len(earlier),
        out_specs=[pl.BlockSpec(memory_space=pltpu.VMEM)] * 2,
        out_shape=[
            pltpu.VMEM((heads, rows, 256), BF),
            pltpu.VMEM((heads, rows, 128), BF),
        ],
        compiler_params=pltpu.CompilerParams(vmem_limit_bytes=KEYS_VMEM),
        cost_estimate=COST,
        name="make_keys",
    )(latent_t, up, *earlier)
    return [pltpu.with_memory_space_constraint(m, pltpu.VMEM) for m in made]


def attend_kernel(info_ref, q_hbm_ref, w_hbm_ref, keys_ref, values_ref, *refs):
    keep_ref, send_ref, q_ref, w_ref, heads_ref, sems = refs[-6:]
    pairs, qb = heads_ref.shape[:2]
    half = qb // 2
    block = info_ref[0]
    core = info_ref[1]
    prefix_len = info_ref[2]
    factor = (NOPE + ROPE) ** (-0.5) * 1.4426950408889634
    ones = jnp.ones((qb, 128), BF)
    fetches = []
    for i, part in enumerate((core, 1 - core)):
        rows = pl.ds(pl.multiple_of(block * qb + part * half, half), half)
        fetches.append(
            pltpu.make_async_copy(q_hbm_ref.at[rows, :], q_ref.at[i * half : (i + 1) * half, :], sems.at[i])
        )
    fetches.append(pltpu.make_async_copy(w_hbm_ref, w_ref, sems.at[2]))
    for fetch in fetches:
        fetch.start()
    for fetch in fetches[:2]:
        fetch.wait()
    prefix_col = lax.broadcasted_iota(jnp.int32, (1, PMAX), 1)
    bias = jnp.where(prefix_col < prefix_len, 0.0, -1e30)

    def one_head(pair, h, count):
        q = q_ref[:, pl.ds(pl.multiple_of(pair * 384 + h * 128, 128), 256)]
        head = pair * 2 + h
        scores = []
        for t in range(PMAX // qb + count):
            s = lax.dot_general(
                q,
                keys_ref[head, t * qb : (t + 1) * qb, :],
                (((1,), (1,)), ((), ())),
                preferred_element_type=F32,
            )
            if t < PMAX // qb:
                s = s + bias[:, t * qb : (t + 1) * qb]
            elif t == PMAX // qb + count - 1:
                col = lax.broadcasted_iota(jnp.int32, (qb, qb), 1)
                row = lax.broadcasted_iota(jnp.int32, (qb, qb), 0)
                s = jnp.where(col <= (row + core * half) % qb, s, -1e30)
            scores.append(s)
        peak = functools.reduce(jnp.maximum, scores)
        peak = jnp.max(peak, 1, keepdims=True)
        total = jnp.zeros((qb, 256), F32)
        for t, s in enumerate(scores):
            p = jnp.exp2((s - peak) * factor).astype(BF)
            v = values_ref[head, t * qb : (t + 1) * qb, :]
            total = total + dot(p, jnp.concatenate([v, ones], 1))
        return (total[:, :128] / total[:, 128:]).astype(BF)

    for b in range(4):

        @pl.when(block == b)
        def _(b=b):
            @pl.loop(0, pairs)
            def _(pair):
                heads_ref[pair, :, :128] = one_head(pair, 0, b + 1)
                heads_ref[pair, :, 128:] = one_head(pair, 1, b + 1)

    attended = jnp.concatenate([heads_ref[i] for i in range(pairs)], 1)
    fetches[2].wait()
    out = dot(attended, w_ref[...])
    keep_ref[...] = out[:half].astype(BF)
    send_ref[...] = out[half:].astype(BF)


def attend_block(info, queries, out_w, made, earlier):
    queries, out_w = [pltpu.with_memory_space_constraint(x, pltpu.HBM) for x in (queries, out_w)]
    heads = made[0].shape[0]
    width = out_w.shape[1]
    qb = 256
    return pl.pallas_call(
        attend_kernel,
        in_specs=[pl.BlockSpec(memory_space=pltpu.SMEM)]
        + [pl.BlockSpec(memory_space=pl.ANY)] * 2
        + [pl.BlockSpec(memory_space=pltpu.VMEM)] * 2
        + [pl.BlockSpec(memory_space=pl.ANY)] * len(earlier),
        out_specs=[pl.BlockSpec(memory_space=pltpu.VMEM)] * 2,
        out_shape=[jax.ShapeDtypeStruct((qb // 2, width), BF)] * 2,
        scratch_shapes=[
            pltpu.VMEM((qb, queries.shape[1]), BF),
            pltpu.VMEM(out_w.shape, BF),
            pltpu.VMEM((heads // 2, qb, 256), BF),
            pltpu.SemaphoreType.DMA((3,)),
        ],
        compiler_params=pltpu.CompilerParams(vmem_limit_bytes=KEYS_VMEM),
        cost_estimate=COST,
        name="attend_block",
    )(info, queries, out_w, *made, *earlier)


def pack(main, extra, spare_ref, msg_refs):
    experts = msg_refs[0].shape[0]
    spare_ref[...] = jnp.zeros_like(spare_ref)
    per = main.shape[1] // 128 // len(msg_refs)
    for i, msg in enumerate(msg_refs):
        for c in range(per):
            lanes = slice((i * per + c) * 128, (i * per + c + 1) * 128)
            msg[:, c * SLOTS : (c + 1) * SLOTS, :] = (
                main[:, lanes].astype(BF).reshape(experts, SLOTS, 128)
            )
            spare_ref[:, i * 16 + c, :] = extra[:, lanes].astype(F32)
        msg[:, per * SLOTS :, :] = spare_ref[:, i * 16 : (i + 1) * 16, :].astype(BF)


def unpack(msg_refs, spare_ref, rows_ref):
    experts = msg_refs[0].shape[0]
    main = experts * SLOTS
    per = rows_ref.shape[1] // 128 // len(msg_refs)
    for i, msg in enumerate(msg_refs):
        spare_ref[:, i * 16 : (i + 1) * 16, :] = msg[:, per * SLOTS :, :].astype(F32)
        for c in range(per):
            lanes = slice((i * per + c) * 128, (i * per + c + 1) * 128)
            rows_ref[:main, lanes] = msg[:, c * SLOTS : (c + 1) * SLOTS, :].reshape(main, 128)
            rows_ref[main : main + experts, lanes] = spare_ref[:, i * 16 + c, :].astype(BF)


def dispatch_kernel(
    hidden_ref, own_ref, own_core_ref, r1_ref, r2_ref, gain_ref, ids_ref, *refs
):
    stream_ref, msg_a_ref, msg_b_ref, spare_ref = refs[-4:]
    rows = hidden_ref.shape[0]
    experts = msg_a_ref.shape[0]
    stream = hidden_ref[...].astype(F32)
    for ref in (own_ref, own_core_ref, r1_ref, r2_ref):
        stream = stream + ref[...].astype(F32)
    stream_ref[...] = stream
    mean = jnp.mean(stream * stream, -1, keepdims=True)
    normed = (stream * lax.rsqrt(mean + 1e-6) * gain_ref[...]).astype(BF)
    before = (
        lax.broadcasted_iota(jnp.int32, (rows, rows), 0)
        < lax.broadcasted_iota(jnp.int32, (rows, rows), 1)
    ).astype(BF)

    def picks(count, expert, slot):
        named = (ids_ref[0:1, :] == expert) | (ids_ref[1:2, :] == expert)
        earlier = dot(named.astype(F32).astype(BF), before)
        return jnp.where(named & (earlier == slot.astype(F32)), 1.0, 0.0).astype(BF)

    line = lax.broadcasted_iota(jnp.int32, (experts * SLOTS, rows), 0)
    main = dot(picks(experts * SLOTS, line // SLOTS, line % SLOTS), normed)
    line = lax.broadcasted_iota(jnp.int32, (experts, rows), 0)
    extra = dot(picks(experts, line, jnp.full((experts, rows), SLOTS, jnp.int32)), normed)
    pack(main, extra, spare_ref, (msg_a_ref, msg_b_ref))


def dispatch(hidden, own, own_core, r1, r2, gain, ids_t, experts, earlier):
    rows, width = hidden.shape
    message = jax.ShapeDtypeStruct((experts, width // 256 * SLOTS + 16, 128), BF)
    return pl.pallas_call(
        dispatch_kernel,
        in_specs=[pl.BlockSpec(memory_space=pltpu.VMEM)] * 7
        + [pl.BlockSpec(memory_space=pl.ANY)] * len(earlier),
        out_shape=[jax.ShapeDtypeStruct((rows, width), F32), message, message],
        scratch_shapes=[pltpu.VMEM((experts, 32, 128), F32)],
        compiler_params=pltpu.CompilerParams(vmem_limit_bytes=VMEM),
        cost_estimate=COST,
        name="dispatch",
    )(hidden, own, own_core, r1, r2, gain.reshape(1, width), ids_t, *earlier)


def expert_kernel(counts, *refs):
    n = len(counts)
    msgs, refs = refs[:2], refs[2:]
    shards = []
    for count in counts:
        shards.append(refs[:count])
        refs = refs[count:]
    outs, refs = refs[:2], refs[2:]
    rows_ref, spare_ref, active_ref, in_buf, out_buf, sems = refs
    cut, width = shards[0][0].shape
    rest = in_buf.shape[1] - cut
    units = out_buf.shape[0] // n
    copies = []
    for s in range(n):
        places = [(shards[s][0], in_buf.at[s, :cut])]
        start = 0
        for piece in shards[s][1:]:
            for row in range(start, start + piece.shape[0], units):
                src = piece.at[row - start : row - start + units]
                if row < rest:
                    dst = in_buf.at[s, cut + row : cut + row + units]
                else:
                    col = (row - rest) // units * width
                    dst = out_buf.at[s * units : (s + 1) * units, col : col + width]
                places.append((src, dst))
            start += piece.shape[0]
        copies.append([pltpu.make_async_copy(*p, sems.at[s, i]) for i, p in enumerate(places)])
        for copy in copies[-1]:
            copy.start()
    unpack(msgs, spare_ref, rows_ref)
    ready = 1 + rest // units
    for s in range(n):
        for copy in copies[s][:ready]:
            copy.wait()
        joined = dot(rows_ref[...], in_buf[s])
        gate, up = joined[:, :units], joined[:, units:]
        active_ref[:, s * units : (s + 1) * units] = (gate / (1.0 + jnp.exp(-gate)) * up).astype(BF)
    for s in range(n):
        for copy in copies[s][ready:]:
            copy.wait()
    total = dot(active_ref[...], out_buf[...])
    experts = outs[0].shape[0]
    main = experts * SLOTS
    pack(total[:main], total[main:], spare_ref, outs)


def run_expert(msgs, shards, depth):
    n = len(shards)
    counts = [len(shard) for shard in shards]
    experts = msgs[0].shape[0]
    cols = shards[0][0].shape[1]
    units = cols // 2
    rows = experts * (SLOTS + 1)
    return pl.pallas_call(
        functools.partial(expert_kernel, counts),
        in_specs=[pl.BlockSpec(memory_space=pltpu.VMEM)] * 2 + [pl.BlockSpec(memory_space=pl.ANY)] * sum(counts),
        out_specs=[pl.BlockSpec(memory_space=pltpu.VMEM)] * 2,
        out_shape=[jax.ShapeDtypeStruct(m.shape, BF) for m in msgs],
        scratch_shapes=[
            pltpu.VMEM((rows, depth), BF),
            pltpu.VMEM((experts, 32, 128), F32),
            pltpu.VMEM((rows, n * units), BF),
            pltpu.VMEM((n, depth, cols), BF),
            pltpu.VMEM((n * units, depth), BF),
            pltpu.SemaphoreType.DMA((n, 1 + (depth - shards[0][0].shape[0]) // units + depth // cols)),
        ],
        compiler_params=pltpu.CompilerParams(vmem_limit_bytes=VMEM),
        cost_estimate=COST,
        name="run_expert",
    )(*msgs, *sum(shards, []))


def combine_kernel(stream_ref, msg_a_ref, msg_b_ref, ids_ref, gates_ref, out_ref, rows_ref, spare_ref):
    rows = stream_ref.shape[0]
    experts = msg_a_ref.shape[0]
    main = experts * SLOTS
    rows_ref[main:, :] = jnp.zeros((128, rows_ref.shape[1]), BF)
    unpack((msg_a_ref, msg_b_ref), spare_ref, rows_ref)
    before = (
        lax.broadcasted_iota(jnp.int32, (rows, rows), 1)
        < lax.broadcasted_iota(jnp.int32, (rows, rows), 0)
    ).astype(BF)
    place = lax.broadcasted_iota(jnp.int32, (rows, main + 128), 1)
    expert = jnp.where(place < main, place // SLOTS, place - main)
    slot = jnp.where(place < main, place % SLOTS, SLOTS)
    first = ids_ref[:, 0:1] == expert
    second = ids_ref[:, 1:2] == expert
    named = jnp.where(first | second, 1.0, 0.0).astype(BF)
    earlier = dot(before, named)
    weight = jnp.where(first, gates_ref[:, 0:1], jnp.where(second, gates_ref[:, 1:2], 0.0))
    weight = jnp.where(earlier == slot.astype(F32), weight, 0.0)
    mix = stream_ref[...]
    for _ in range(3):
        part = weight.astype(BF)
        mix = mix + dot(part, rows_ref[...])
        weight = weight - part.astype(F32)
    out_ref[...] = mix.astype(BF)


def combine(stream, msgs, ids, gates):
    rows, width = stream.shape
    experts = msgs[0].shape[0]
    return pl.pallas_call(
        combine_kernel,
        out_shape=jax.ShapeDtypeStruct((rows, width), BF),
        scratch_shapes=[
            pltpu.VMEM((experts * SLOTS + 128, width), BF),
            pltpu.VMEM((experts, 32, 128), F32),
        ],
        compiler_params=pltpu.CompilerParams(vmem_limit_bytes=VMEM),
        cost_estimate=COST,
        name="combine",
    )(stream, *msgs, ids, gates)


def shards(
    hidden_in,
    query_heads,
    latent_cache,
    prefix_lens,
    latent_up,
    head_out,
    norm_gain,
    expert_ids,
    gate_weights,
    expert_in,
    expert_out,
):
    experts = lax.axis_size("dp")
    group = lax.axis_size("ep")
    chips = group // 2
    place = lax.axis_index("ep")
    chip, core = place // 2, place % 2

    def to_chip(x, target):
        pairs = [(i, 2 * target(i // 2) + i % 2) for i in range(group)]
        return lax.ppermute(x, "ep", pairs)

    def to_core(x):
        return lax.ppermute(x, "ep", [(i, i ^ 1) for i in range(group)])

    pair = lambda x: x ^ 1
    other = lambda x: chips - 1 - x
    depth = expert_in.shape[1]
    cut = 2304
    first = expert_in[0, :cut].reshape(cut, -1)
    first_pair, first_core = to_chip(first, pair), to_core(first)

    made = make_keys(latent_cache[0].T, latent_up, [first])

    def attend(target, earlier):
        info = jnp.stack([target, core, prefix_lens[0]]).astype(jnp.int32)
        keep, send = attend_block(info, query_heads, head_out, made, earlier)
        return keep, to_core(send)

    def add(*terms):
        return sum(t.astype(F32) for t in terms).astype(BF)

    far = attend(pair(other(chip)), [])
    far_sum = add(*far)
    near = attend(other(chip), [far[0]])
    far_in = to_chip(far_sum, other)
    side = attend(pair(chip), [near[0], far_sum])
    near_sum = add(*near)
    near_in = to_chip(near_sum, other)
    own = attend(chip, [side[0], near_sum, first_pair])
    side_in = to_chip(add(*side, far_in), pair)

    rest_in, rest_out, _ = lax.optimization_barrier((expert_in[0, cut:], expert_out[0], own[0]))
    cols = first.shape[1]
    second = [rest_in.reshape(depth - cut, cols)]
    second = jnp.concatenate(second + [rest_out[:, i : i + cols] for i in range(0, depth, cols)], 0)
    second, near_in, side_in = lax.optimization_barrier((second, near_in, side_in))
    second_pair, second_core = to_chip(second, pair), to_core(second)
    first_across = to_core(first_pair)
    stream, *msgs = dispatch(
        hidden_in, *own, near_in, side_in, norm_gain, expert_ids.T, experts, [first_across, first_core]
    )
    exchange = lambda m: lax.all_to_all(m, "dp", split_axis=0, concat_axis=0, tiled=True)
    mine = [exchange(m) for m in msgs]
    theirs = [to_chip(m, other) for m in mine]
    theirs[0], mine[1], second_pair, second_core = lax.optimization_barrier(
        (theirs[0], mine[1], second_pair, second_core)
    )
    step = second_pair.shape[0] // 4
    second_across = [to_core(second_pair[i : i + step]) for i in range(0, 4 * step, step)]
    weights = [[first, second], [first_core, second_core]]
    weights += [[first_pair, second_pair], [first_across, *second_across]]
    theirs_out = run_expert(theirs, weights, depth)
    mine_out = run_expert(mine, weights, depth)
    back = [to_chip(m, other) for m in theirs_out]
    home = [exchange(add(a, b)) for a, b in zip(mine_out, back)]
    return combine(stream, home, expert_ids, gate_weights)


def solution(mesh):
    in_specs = (
        P(("dp", "ep"), None),
        P("dp", "ep"),
        P("dp", None, None),
        P("dp"),
        P(None, "ep"),
        P("ep", None),
        P(),
        P(("dp", "ep"), None),
        P(("dp", "ep"), None),
        P("dp", None, None, "ep"),
        P("dp", "ep", None),
    )
    out_specs = P(("dp", "ep"), None)
    return jax.shard_map(shards, mesh=mesh, in_specs=in_specs, out_specs=out_specs, check_vma=False)
```
